32 devices in a mesh: dp: 8 (over z, y), expert: 4 (over x, core).
Axes of the slice: x: 2, y: 2, z: 4, core: 2. Of those that a mesh axis runs over, the one named last changes fastest.
Arguments:
- tokens: bfloat16 [16, 1024, 2048], P('dp', 'expert'), may hold values from -6 to 6
- lengths: int32 [16], P('dp'), may hold values from 256 to 1024, as said below
- routes: int32 [8, 4, 512, 8], P('dp', 'expert'), may hold values from 0 to 15, all different within a row; in each aligned block of 512 rows (0 to 511, 512 to 1023, ..., all dimensions but the last counted through in order) at most 288 rows name the same one
- w_query: bfloat16 [2048, 2048], P(('dp', 'expert')), may hold values from -0.125 to 0.125
- w_key: bfloat16 [2048, 2048], P(('dp', 'expert')), may hold values from -0.125 to 0.125
- w_value: bfloat16 [2048, 2048], P(('dp', 'expert')), may hold values from -0.125 to 0.125
- w_out: bfloat16 [2048, 2048], P(('dp', 'expert')), may hold values from -1.5 to 1.5
- w_router: bfloat16 [2048, 16], P(('dp', 'expert')), may hold values from -0.0625 to 0.0625
- attn_gain: bfloat16 [2048], P(('dp', 'expert')), may hold values from 0.099609375 to 1.8984375
- query_gain: bfloat16 [2048], P(('dp', 'expert')), may hold values from 0.099609375 to 1.8984375
- key_gain: bfloat16 [2048], P(('dp', 'expert')), may hold values from 0.099609375 to 1.8984375
- ffn_gain: bfloat16 [2048], P(('dp', 'expert')), may hold values from 0.099609375 to 1.8984375
- w_gate: bfloat16 [16, 2048, 1024], P('expert'), may hold values from -0.125 to 0.125
- w_up: bfloat16 [16, 2048, 1024], P('expert'), may hold values from -0.125 to 0.125
- w_down: bfloat16 [16, 1024, 2048], P('expert'), may hold values from -2 to 2
- cotangent: bfloat16 [16, 1024, 2048], P('dp', 'expert'), may hold values from -6 to 6
Outputs:
- output: bfloat16 [16, 1024, 2048], P('dp', 'expert')
- grad_input: float32 [16, 1024, 2048], P('dp', 'expert')
- grad_query: float32 [2048, 2048], P(('dp', 'expert'))
- grad_key: float32 [2048, 2048], P(('dp', 'expert'))
- grad_value: float32 [2048, 2048], P(('dp', 'expert'))
- grad_outproj: float32 [2048, 2048], P(('dp', 'expert'))
- grad_router: float32 [2048, 16], P(('dp', 'expert'))
- grad_attn_gain: float32 [2048], P(('dp', 'expert'))
- grad_query_gain: float32 [2048], P(('dp', 'expert'))
- grad_key_gain: float32 [2048], P(('dp', 'expert'))
- grad_ffn_gain: float32 [2048], P(('dp', 'expert'))
- grad_gate: float32 [16, 2048, 1024], P('expert', 'dp')
- grad_up: float32 [16, 2048, 1024], P('expert', 'dp')
- grad_down: float32 [16, 1024, 2048], P('expert', None, 'dp')
The draws below stay inside these ranges and needn't reach their ends.
Inputs may be any that keep to these rules, and one draw needn't show every extreme that they name: `lengths`: in each data group one of its 2 sequences, chosen by the seed, has length 1024. Each token names 8 different experts; within the 512 tokens of one block routes[g,b] no expert is named more than 288 times, a bound that some block reaches.
All inputs are finite; a program needn't handle non-finite values.
Results may differ from the reference program's by a relative error of at most 0.02.
Values may be sent and summed in bfloat16 or wider, within the bound.
A program may use at most 512 MiB of HBM per device.

```python
import math
import jax
import jax.numpy as jnp
import numpy as np
from jax import lax

D = 2048
HEADS = 16
HEAD_DIM = 128
FF = 1024
EXPERTS = 16
TOP = 8
SEQ_GROUP = 2
LEN = 1024
SEQS = 16
TOK_DEV = 512
CAP = 288
N_DP = 8
N_EXPERT = 4


def draw_lengths(key, part):
    groups = SEQS // SEQ_GROUP
    first_key, second_key = jax.random.split(key)
    full_index = jax.random.randint(first_key, (groups, 1), 0, SEQ_GROUP)
    ragged_len = jax.random.randint(second_key, (groups, SEQ_GROUP), LEN // 4, LEN + 1)
    seq_index = jnp.arange(SEQ_GROUP, dtype=jnp.int32)[None, :]
    return jnp.where(seq_index == full_index, LEN, ragged_len).reshape(SEQS).astype(jnp.int32)


def block_levels(own_key, dims, pieces, smallest, high):
    gain, own = 1.0, jax.random.fold_in(own_key, 6)
    for dim, parts in pieces:
        heights = jnp.exp(jax.random.uniform(jax.random.fold_in(own, dim), (parts,), jnp.float32, smallest / len(pieces), high / len(pieces)))
        gain = gain * jnp.repeat(heights, dims[dim] // parts).reshape([-1 if axis == dim else 1 for axis in range(len(dims))])
    return gain


def assign_block(key, own, number, rows, number_of, top, reach, skew):
    sequence = jax.random.permutation(key, number_of)
    heavy_load, common = load_shares(number_of, rows * top, reach, skew, True), load_shares(number_of, rows * top, reach, skew, False)
    places = jnp.arange(number_of)

    def named(sizes, rotation):
        used = int((sizes > 0).sum())
        fixed = max(1, used // 4)
        moved = fixed + (places - fixed + rotation * (used - fixed)) % max(1, number_of - fixed)
        return jnp.zeros((number_of,), jnp.int32).at[sequence[jnp.where(places < fixed, places, moved)]].set(jnp.asarray(sizes, jnp.int32))

    sizes = jnp.where(number % 4 == 0, named(heavy_load, number // 4), named(common, number - number // 4 - 1))
    mixed = jax.random.permutation(jax.random.fold_in(own, 3), number_of)
    source_of, receiver = mixed[0:number_of // 2 * 2:2], mixed[1:number_of // 2 * 2:2]
    room = jnp.minimum(sizes[source_of] - 1, reach - sizes[receiver]) // 2
    room = jnp.where((source_of == sequence[0]) | (receiver == sequence[0]) | (sizes[receiver] == 0), 0, jnp.maximum(room, 0))
    moved = jax.random.randint(jax.random.fold_in(own, 4), (number_of // 2,), 0, 1 << 20) % (room + 1)
    sizes = sizes.at[source_of].add(-moved).at[receiver].add(moved)
    items = jnp.searchsorted(jnp.cumsum(sizes), jnp.arange(rows * top), side="right").astype(jnp.int32)
    grid = items.reshape(top, rows).T
    grid = grid[jax.random.permutation(jax.random.fold_in(own, 1), rows)]
    rotation = jax.random.randint(jax.random.fold_in(own, 2), (rows, 1), 0, top)
    return jnp.take_along_axis(grid, (jnp.arange(top)[None, :] + rotation) % top, axis=1)


def load_shares(number_of, total, bound, slope, full):
    portions = [(1 << 20) // math.isqrt(grade ** slope) + 1 for grade in range(1, number_of + 1)]
    largest = bound if full else min(bound, max(-(-total // number_of), total * portions[0] // sum(portions)))
    least = 1 if total - largest >= number_of - 1 else 0
    given, rest = [largest] + [least] * (number_of - 1), total - largest - least * (number_of - 1)
    while rest > 0:
        candidates = [i for i in range(1, number_of) if given[i] < largest] or [i for i in range(1, number_of) if given[i] < bound]
        mass, left = sum([portions[i] for i in candidates]), rest
        for i in candidates:
            more = min(bound - given[i], max(1, left * portions[i] // mass), rest)
            given[i] = given[i] + more
            rest = rest - more
    return np.array(given)


def centred(own_key, dims, deviation, bound, cuts=(), kind=jnp.bfloat16):
    drawn = deviation * jax.random.normal(own_key, dims, jnp.float32)
    if cuts:
        drawn = drawn * block_levels(own_key, dims, cuts, -0.22, 0.18)
    return jnp.clip(drawn, -bound, bound).astype(kind)


def setup_inputs(seed: int = 0) -> dict:
    seeds = jax.random.split(jax.random.key(seed), 17)
    tokens = centred(seeds[0], (SEQS, LEN, D), 1.0, 6.0, ((0, 8), (1, 4)))
    lengths = draw_lengths(jax.random.fold_in(seeds[16], 71), 0)
    routes_keys = jax.random.split(jax.random.fold_in(seeds[2], 1), N_DP * N_EXPERT * TOK_DEV // TOK_DEV)
    routes_turns = jax.random.permutation(jax.random.fold_in(seeds[2], 3), N_DP * N_EXPERT * TOK_DEV // TOK_DEV)
    routes = jax.vmap(lambda own, number: assign_block(jax.random.fold_in(seeds[2], 2), own, number, TOK_DEV, EXPERTS, TOP, CAP, 1))(routes_keys, routes_turns).reshape((N_DP, N_EXPERT, TOK_DEV, TOP))
    w_query = centred(seeds[3], (D, D), D ** -0.5, 0.125, ((0, 32),))
    w_key = centred(seeds[4], (D, D), D ** -0.5, 0.125, ((0, 32),))
    w_value = centred(seeds[5], (D, D), D ** -0.5, 0.125, ((0, 32),))
    w_out = centred(seeds[6], (D, D), (D * 8 // LEN) ** -0.5, 1.5, ((0, 32),))
    w_router = centred(seeds[7], (D, EXPERTS), (4 * D) ** -0.5, 0.0625, ((0, 32),))
    attn_gain = jnp.clip(1.0 + 0.18 * jax.random.normal(seeds[8], (D,), jnp.float32), 0.099609375, 1.8984375).astype(jnp.bfloat16)
    query_gain = jnp.clip(1.0 + 0.18 * jax.random.normal(seeds[9], (D,), jnp.float32), 0.099609375, 1.8984375).astype(jnp.bfloat16)
    key_gain = jnp.clip(1.0 + 0.18 * jax.random.normal(seeds[10], (D,), jnp.float32), 0.099609375, 1.8984375).astype(jnp.bfloat16)
    ffn_gain = jnp.clip(1.0 + 0.18 * jax.random.normal(seeds[11], (D,), jnp.float32), 0.099609375, 1.8984375).astype(jnp.bfloat16)
    w_gate = centred(seeds[12], (EXPERTS, D, FF), D ** -0.5, 0.125, ((0, 4),))
    w_up = centred(seeds[13], (EXPERTS, D, FF), D ** -0.5, 0.125, ((0, 4),))
    w_down = centred(seeds[14], (EXPERTS, FF, D), (max(1, FF // 128)) ** -0.5, 2.0, ((0, 4),))
    cotangent = centred(seeds[15], (SEQS, LEN, D), 1.0, 6.0, ((0, 8), (1, 4)))
    return {"tokens": tokens, "lengths": lengths, "routes": routes, "w_query": w_query, "w_key": w_key, "w_value": w_value, "w_out": w_out, "w_router": w_router, "attn_gain": attn_gain, "query_gain": query_gain, "key_gain": key_gain, "ffn_gain": ffn_gain, "w_gate": w_gate, "w_up": w_up, "w_down": w_down, "cotangent": cotangent}


@jax.custom_vjp
def low(v):
    return lax.optimization_barrier(v.astype(jnp.bfloat16)).astype(jnp.float32)

@jax.custom_vjp
def low_back(v):
    return v

def low_keep(v):
    return (low(v), None)

def low_pass(kept, grad):
    return (grad,)

def back_keep(v):
    return (v, None)

def back_low(kept, grad):
    return (low(grad),)
low.defvjp(low_keep, low_pass)
low_back.defvjp(back_keep, back_low)
epsilon = 1e-05
highest = lax.Precision.HIGHEST

def matmul(left_side, right_side):
    return jnp.dot(left_side, right_side, precision=highest)

def rms_scale(values, gain_vector):
    factor = lax.rsqrt(lax.optimization_barrier(jnp.mean(values * values, axis=-1, keepdims=True)) + epsilon)
    return values * factor * gain_vector

def rotary(values, positions):
    half_dim = values.shape[-1] // 2
    frequencies = jnp.exp(jnp.arange(half_dim, dtype=jnp.float32) * (-2.0 * math.log(10000.0) / values.shape[-1]))
    angles = positions.astype(jnp.float32)[:, None] * frequencies[None, :]
    cosine = jnp.cos(angles)[:, None, :]
    sine_part = jnp.sin(angles)[:, None, :]
    first_half = values[..., :half_dim]
    second = values[..., half_dim:]
    return jnp.concatenate([first_half * cosine - second * sine_part, second * cosine + first_half * sine_part], axis=-1)

def softmax_rows(scores):
    row_peak = lax.optimization_barrier(jnp.max(scores, axis=-1, keepdims=True))
    exponent = jnp.exp(scores - row_peak)
    return exponent / lax.optimization_barrier(jnp.sum(exponent, axis=-1, keepdims=True))

def group_forward(tokens, lengths, routes, w_query, w_key, w_value, w_out, w_router, attn_gain, query_gain, key_gain, ffn_gain, w_gate, w_up, w_down):
    seq_count, seq_length, model_width = tokens.shape
    block_count, block_tokens, top_count = routes.shape
    span_dev = seq_length // block_count
    experts = w_gate.shape[0]
    capacity = CAP
    score_scale = 1.0 / math.sqrt(HEAD_DIM)
    flat_tokens = tokens.reshape(seq_count * seq_length, model_width)
    normed = low(rms_scale(flat_tokens, attn_gain))
    query_raw = low_back(matmul(normed, w_query))
    key_raw = low_back(matmul(normed, w_key))
    value_raw = matmul(normed, w_value)
    places = jnp.tile(jnp.arange(seq_length, dtype=jnp.int32), seq_count)
    query = low(rotary(rms_scale(query_raw, query_gain).reshape(-1, HEADS, HEAD_DIM), places))
    query = query.reshape(seq_count, seq_length, HEADS, HEAD_DIM)
    keyed = low(rotary(rms_scale(key_raw, key_gain).reshape(-1, HEADS, HEAD_DIM), places))
    keyed = keyed.reshape(seq_count, seq_length, HEADS, HEAD_DIM)
    values = low(low_back(value_raw)).reshape(seq_count, seq_length, HEADS, HEAD_DIM)
    scores = low_back(jnp.einsum('sqhd,skhd->shqk', query, keyed, precision=highest) * score_scale)
    position = jnp.arange(seq_length, dtype=jnp.int32)
    allowed = (position[None, :] <= position[:, None])[None, None] & (position[None, None, None, :] < lengths[:, None, None, None])
    attn_probs = softmax_rows(jnp.where(allowed, scores, -1e+30))
    attended = jnp.einsum('shqk,skhd->sqhd', low(attn_probs), values, precision=highest)
    attended = low(low_back(attended.reshape(seq_count * seq_length, model_width)))
    resid = flat_tokens + low_back(matmul(attended, w_out))
    ffn_in = low(rms_scale(resid, ffn_gain))
    router = softmax_rows(matmul(ffn_in, w_router))

    def to_blocks(array):
        return array.reshape(seq_count, block_count, span_dev, -1).transpose(1, 0, 2, 3).reshape(block_count, seq_count * span_dev, -1)
    ffn_blocks = to_blocks(ffn_in)
    router_blocks = to_blocks(router)
    gate_weight = jnp.take_along_axis(router_blocks, routes, axis=-1)
    pair_expert = routes.reshape(block_count, block_tokens * top_count)
    onehot = (pair_expert[:, :, None] == jnp.arange(experts, dtype=jnp.int32)).astype(jnp.int32)
    before = jnp.cumsum(onehot, axis=1) - onehot
    rank = lax.optimization_barrier(jnp.sum(before * onehot, axis=-1))
    block_index = jnp.arange(block_count, dtype=jnp.int32)[:, None]
    slot = (pair_expert * (block_count * capacity) + block_index * capacity + rank).reshape(-1)
    source = (block_index * block_tokens + jnp.arange(block_tokens * top_count, dtype=jnp.int32)[None, :] // top_count).reshape(-1)
    owner = jnp.full((experts * block_count * capacity,), block_count * block_tokens, jnp.int32).at[slot].set(source)
    padded = jnp.concatenate([ffn_blocks.reshape(block_count * block_tokens, model_width), jnp.zeros((1, model_width), jnp.float32)], axis=0)
    buffer = low_back(padded[owner].reshape(experts, block_count * capacity, model_width))
    gate_proj = low_back(jnp.einsum('erd,edf->erf', buffer, w_gate, precision=highest))
    up_proj = low_back(jnp.einsum('erd,edf->erf', buffer, w_up, precision=highest))
    hidden = low(gate_proj * jax.nn.sigmoid(gate_proj) * up_proj)
    expert_out = low(low_back(jnp.einsum('erf,efd->erd', hidden, w_down, precision=highest)))
    expert_rows = expert_out.reshape(-1, model_width)[slot].reshape(block_count, block_tokens, top_count, model_width)
    mixture = jnp.einsum('btk,btkd->btd', gate_weight, expert_rows, precision=highest)
    mixture = mixture.reshape(block_count, seq_count, span_dev, model_width).transpose(1, 0, 2, 3).reshape(seq_count * seq_length, model_width)
    return (resid + mixture).reshape(seq_count, seq_length, model_width)

def reference(tokens, lengths, routes, w_query, w_key, w_value, w_out, w_router, attn_gain, query_gain, key_gain, ffn_gain, w_gate, w_up, w_down, cotangent):
    weights = tuple((array.astype(jnp.float32) for array in (w_query, w_key, w_value, w_out, w_router, attn_gain, query_gain, key_gain, ffn_gain, w_gate, w_up, w_down)))
    all_tokens = tokens.astype(jnp.float32).reshape(N_DP, SEQ_GROUP, LEN, D)
    all_cot = cotangent.astype(jnp.float32).reshape(N_DP, SEQ_GROUP, LEN, D)
    all_lengths = lengths.reshape(N_DP, SEQ_GROUP)

    def one_group(running, group_items):
        group_tokens, group_lengths, group_routes, group_cot = group_items

        def forward(token_values, *weight_values):
            return group_forward(token_values, group_lengths, group_routes, *weight_values)
        result, pullback = jax.vjp(forward, group_tokens, *weights)
        valid_mask = (jnp.arange(LEN, dtype=jnp.int32)[None, :] < group_lengths[:, None]).astype(jnp.float32)
        grads = pullback(group_cot * valid_mask[:, :, None])
        running = tuple((acc + grad for acc, grad in zip(running, grads[1:])))
        return (running, (result.astype(jnp.bfloat16), grads[0]))
    start = tuple((jnp.zeros_like(array) for array in weights))
    sums, (results, input_grads) = lax.scan(one_group, start, (all_tokens, all_lengths, routes, all_cot))
    return (results.reshape(SEQS, LEN, D), input_grads.reshape(SEQS, LEN, D), sums[0], sums[1], sums[2], sums[3], sums[4], sums[5], sums[6], sums[7], sums[8], sums[9], sums[10], sums[11])
```

```python
from functools import partial
import math

import jax
import jax.numpy as jnp
from jax import lax
from jax.experimental import pallas as pl
from jax.experimental.pallas import tpu as pltpu
from jax.sharding import Mesh, PartitionSpec as P

HEAD_DIM = 128
EXPERTS = 16
EPS = 1e-05
F32 = jnp.float32
BF = jnp.bfloat16
VMEM_LIMIT = 60 * 1024 * 1024


def dot(a, b, dims=((1,), (0,))):
    return lax.dot_general(a, b, (dims, ((), ())), preferred_element_type=F32)


NT = ((1,), (1,))
TN = ((0,), (0,))


def masked_scores(q, k, i, j, rows, length, scale):
    s = dot(q, k, NT) * scale
    col = j * rows + lax.broadcasted_iota(jnp.int32, s.shape, 1)
    ok = col < length
    if i == j:
        row = i * rows + lax.broadcasted_iota(jnp.int32, s.shape, 0)
        ok = ok & (col <= row)
    return jnp.where(ok, s, -1e30)


def probs_of(q, k_ref, inv, i, rows, length, scale):
    parts = [
        masked_scores(q, k_ref[inv[j]], i, j, rows, length, scale) for j in range(i + 1)
    ]
    peak = parts[0].max(axis=1, keepdims=True)
    for s in parts[1:]:
        peak = jnp.maximum(peak, s.max(axis=1, keepdims=True))
    parts = [jnp.exp(s - peak) for s in parts]
    total = parts[0].sum(axis=1, keepdims=True)
    for e in parts[1:]:
        total = total + e.sum(axis=1, keepdims=True)
    inverse = 1.0 / total
    return [e * inverse for e in parts]


def attend_kernel(inv, lens, q_ref, k_ref, v_ref, o_ref, *, blocks, rows, scale):
    length = lens[pl.program_id(0)]
    for i in range(blocks):
        probs = probs_of(q_ref[inv[i]], k_ref, inv, i, rows, length, scale)
        out = jnp.zeros((rows, HEAD_DIM), F32)
        for j, p in enumerate(probs):
            out = out + dot(p.astype(BF), v_ref[inv[j]])
        o_ref[i] = out.astype(BF)


def attend_back_kernel(
    inv, lens, q_ref, k_ref, v_ref, do_ref, dq_ref, dk_ref, dv_ref, dk_acc, dv_acc, *, blocks, rows, scale
):
    length = lens[pl.program_id(0)]
    dk_acc[...] = jnp.zeros_like(dk_acc)
    dv_acc[...] = jnp.zeros_like(dv_acc)
    for i in range(blocks):
        q = q_ref[inv[i]]
        do = do_ref[i]
        probs = probs_of(q, k_ref, inv, i, rows, length, scale)
        dprobs = [dot(do, v_ref[inv[j]], NT) for j in range(i + 1)]
        delta = jnp.zeros((rows, 1), F32)
        for p, dp in zip(probs, dprobs):
            delta = delta + jnp.sum(p * dp, axis=1, keepdims=True)
        dq = jnp.zeros((rows, HEAD_DIM), F32)
        for j, (p, dp) in enumerate(zip(probs, dprobs)):
            ds = (p * (dp - delta)).astype(BF)
            dq = dq + dot(ds, k_ref[inv[j]])
            dk_acc[j] += dot(ds, q, TN)
            dv_acc[j] += dot(p.astype(BF), do, TN)
        dq_ref[inv[i]] = dq * scale
    for j in range(blocks):
        dk_ref[inv[j]] = dk_acc[j] * scale
        dv_ref[inv[j]] = dv_acc[j].astype(BF)


def attention_call(kernel, inv, lens, ins, out_types, scratch, flops):
    blocks, seqs, rows, width = ins[0].shape
    heads = width // HEAD_DIM
    spec = pl.BlockSpec((blocks, None, rows, HEAD_DIM), lambda s, h, *_: (0, s, 0, h))
    return pl.pallas_call(
        partial(kernel, blocks=blocks, rows=rows, scale=1.0 / math.sqrt(HEAD_DIM)),
        out_shape=[jax.ShapeDtypeStruct(ins[0].shape, t) for t in out_types],
        grid_spec=pltpu.PrefetchScalarGridSpec(
            num_scalar_prefetch=2,
            grid=(seqs, heads),
            in_specs=[spec] * len(ins),
            out_specs=[spec] * len(out_types),
            scratch_shapes=scratch,
        ),
        compiler_params=pltpu.CompilerParams(vmem_limit_bytes=VMEM_LIMIT),
        cost_estimate=pl.CostEstimate(
            flops=flops, bytes_accessed=ins[0].size * 8, transcendentals=blocks * rows * blocks * rows * seqs * heads
        ),
    )(inv, lens, *ins)


def pick_row(table, index):
    which = lax.broadcasted_iota(jnp.int32, table.shape, 0) == index
    return jnp.sum(jnp.where(which, table, 0.0), axis=0, keepdims=True)


def experts_in_kernel(
    base, f00, f01, f10, f11, c00, c01, c10, c11, r0, r1, g0, g1, wg, wu, wd, *rest, cap, aliased
):
    buf, og, hg, dg, du, gg, weight, dots = rest[5 if aliased else 0 :]
    e, f = pl.program_id(0), pl.program_id(1)
    expert = base[1] + e
    half = f00.shape[0]

    def select(b):
        rank = pick_row((r0, r1)[b][...], expert)
        slot = lax.broadcasted_iota(jnp.int32, (cap, rank.shape[1]), 0).astype(F32)
        return slot == rank

    @pl.when(f == 0)
    def _():
        for b in range(2):
            s = select(b)
            sb = s.astype(F32).astype(BF)
            rows = pl.ds(b * cap, cap)
            top, low = ((f00, f01), (f10, f11))[b]
            buf[rows, :] = (dot(sb[:, :half], top[...]) + dot(sb[:, half:], low[...])).astype(BF)
            top, low = ((c00, c01), (c10, c11))[b]
            og[rows, :] = (dot(sb[:, :half], top[...]) + dot(sb[:, half:], low[...])).astype(BF)
            gate = pick_row((g0, g1)[b][...], expert)
            weight[rows, :] = jnp.sum(jnp.where(s, gate, 0.0), axis=1, keepdims=True)
        dots[...] = jnp.zeros_like(dots)

    x, o = buf[...], og[...]
    gate = dot(x, wg[...])
    up = dot(x, wu[...])
    dh = dot(o, wd[...], NT)
    w = weight[...]
    sg = 1.0 / (1.0 + jnp.exp(-gate))
    silu = gate * sg
    hidden = (silu * up).astype(BF).astype(F32)
    dots[...] += jnp.sum(hidden * dh, axis=1, keepdims=True)
    dh = dh * w
    hg[...] = (hidden * w).astype(BF)
    dg[...] = (dh * up * (sg * (1.0 + gate * (1.0 - sg)))).astype(BF)
    du[...] = (dh * silu).astype(BF)

    @pl.when(f == pl.num_programs(1) - 1)
    def _():
        for b in range(2):
            s = select(b)
            gg[b] = jnp.sum(jnp.where(s, dots[pl.ds(b * cap, cap), :], 0.0), axis=0, keepdims=True)


def experts_in(group, groups, base, feats, cots, ranks, gates, wg, wu, wd, cap, local, before):
    tokens = ranks[0].shape[1]
    width, ff = wg.shape[1:]
    tile = 512
    whole = lambda a: pl.BlockSpec(a.shape, lambda e, f, s: (0, 0), pipeline_mode=pl.Buffered(1))
    small = [*feats, *cots, *ranks, *gates]
    rows = 2 * cap
    wide = pl.BlockSpec((None, rows, width), lambda e, f, s: (e, group, 0))
    thin = pl.BlockSpec((None, rows, tile), lambda e, f, s: (e, group, f))
    wide_type = jax.ShapeDtypeStruct((local, groups * rows, width), BF)
    thin_type = jax.ShapeDtypeStruct((local, groups * rows, ff), BF)
    aliased = before is not None
    n = 1 + len(small) + 3
    return pl.pallas_call(
        partial(experts_in_kernel, cap=cap, aliased=aliased),
        out_shape=[wide_type, wide_type, thin_type, thin_type, thin_type, jax.ShapeDtypeStruct((local, 2, 1, tokens), F32)],
        grid_spec=pltpu.PrefetchScalarGridSpec(
            num_scalar_prefetch=1,
            grid=(local, ff // tile),
            in_specs=[whole(a) for a in small]
            + [
                pl.BlockSpec((None, width, tile), lambda e, f, s: (s[0] + e, 0, f)),
                pl.BlockSpec((None, width, tile), lambda e, f, s: (s[0] + e, 0, f)),
                pl.BlockSpec((None, tile, width), lambda e, f, s: (s[0] + e, f, 0)),
            ]
            + [pl.BlockSpec(memory_space=pl.ANY)] * (5 if aliased else 0),
            out_specs=[wide, wide, thin, thin, thin, pl.BlockSpec((None, 2, 1, tokens), lambda e, f, s: (e, 0, 0, 0))],
            scratch_shapes=[pltpu.VMEM((rows, 1), F32), pltpu.VMEM((rows, 1), F32)],
        ),
        input_output_aliases={n + i: i for i in range(5)} if aliased else {},
        compiler_params=pltpu.CompilerParams(vmem_limit_bytes=VMEM_LIMIT),
        cost_estimate=pl.CostEstimate(
            flops=local * rows * width * (6 * ff + 4 * tokens),
            bytes_accessed=local * (3 * width * ff + rows * (2 * width + 3 * ff)) * 2 + 8 * tokens * width,
            transcendentals=local * rows * ff,
        ),
    )(base, *small, wg, wu, wd, *(before if aliased else ()))


def experts_out_kernel(base, hg, dg, du, r0, r1, wg, wu, wd, m0, m1, d0, d1, *accs, cap):
    e = pl.program_id(1)
    expert = base[1] + e
    out = dot(hg[e], wd[...]).astype(BF)
    back = (dot(dg[e], wg[...], NT) + dot(du[e], wu[...], NT)).astype(BF)
    for b, (rank, mix, dff) in enumerate(((r0, m0, d0), (r1, m1, d1))):
        table = rank[...]
        which = lax.broadcasted_iota(jnp.int32, table.shape, 1) == expert
        column = jnp.sum(jnp.where(which, table, 0.0), axis=1, keepdims=True)
        slot = lax.broadcasted_iota(jnp.int32, (table.shape[0], cap), 1).astype(F32)
        s = (slot == column).astype(F32).astype(BF)
        rows = slice(b * cap, (b + 1) * cap)
        for acc, value, final in ((accs[2 * b], out, mix), (accs[2 * b + 1], back, dff)):
            term = dot(s, value[rows])

            @pl.when(e == 0)
            def _():
                acc[...] = term

            @pl.when(e > 0)
            def _():
                acc[...] += term

            @pl.when(e == pl.num_programs(1) - 1)
            def _():
                final[...] = acc[...].astype(BF)


def experts_out(group, base, hg, dg, du, ranks, wg, wu, wd, cap, local):
    tokens = ranks[0].shape[0]
    width, ff = wg.shape[1:]
    tile = 512
    rows = 2 * cap
    thin = pl.BlockSpec((local, rows, ff), lambda d, e, s: (0, group, 0))
    whole = pl.BlockSpec((tokens, EXPERTS), lambda d, e, s: (0, 0))
    final = pl.BlockSpec((tokens, tile), lambda d, e, s: (0, d))
    return pl.pallas_call(
        partial(experts_out_kernel, cap=cap),
        out_shape=[jax.ShapeDtypeStruct((tokens, width), BF)] * 4,
        grid_spec=pltpu.PrefetchScalarGridSpec(
            num_scalar_prefetch=1,
            grid=(width // tile, local),
            in_specs=[
                thin,
                thin,
                thin,
                whole,
                whole,
                pl.BlockSpec((None, tile, ff), lambda d, e, s: (s[0] + e, d, 0)),
                pl.BlockSpec((None, tile, ff), lambda d, e, s: (s[0] + e, d, 0)),
                pl.BlockSpec((None, ff, tile), lambda d, e, s: (s[0] + e, 0, d)),
            ],
            out_specs=[final] * 4,
            scratch_shapes=[pltpu.VMEM((tokens, tile), F32)] * 4,
        ),
        compiler_params=pltpu.CompilerParams(vmem_limit_bytes=VMEM_LIMIT),
        cost_estimate=pl.CostEstimate(
            flops=local * rows * width * (6 * ff + 4 * tokens),
            bytes_accessed=local * (3 * width * ff + rows * 3 * ff) * 2 + 8 * tokens * width,
            transcendentals=0,
        ),
    )(base, hg, dg, du, *ranks, wg, wu, wd)


def shift(value, axis, by):
    n = lax.axis_size(axis)
    return lax.ppermute(value, axis, [(i, (i + by) % n) for i in range(n)])


def add_low(*terms):
    total = terms[0].astype(F32)
    for t in terms[1:]:
        total = total + t.astype(F32)
    return total.astype(BF)


def rms_parts(values):
    return values * lax.rsqrt(jnp.mean(values * values, axis=-1, keepdims=True) + EPS)


def local(
    nx,
    tokens,
    lengths,
    routes,
    w_query,
    w_key,
    w_value,
    w_out,
    w_router,
    attn_gain,
    query_gain,
    key_gain,
    ffn_gain,
    w_gate,
    w_up,
    w_down,
    cotangent,
):
    ALL, GROUP = ("r", "y", "x", "c"), ("x", "c")
    r, y, x, c = (lax.axis_index(a) for a in ALL)
    nr = lax.axis_size("r")
    me = 2 * x + c
    ng = 2 * nx
    seqs, span, width = tokens.shape
    token_count = seqs * span
    top_count = routes.shape[-1]
    cap = (token_count * top_count * 9 + 8 * EXPERTS - 1) // (8 * EXPERTS)
    cols = width // ng
    length = span * ng
    places = [(dx, dc) for dx in range(nx) for dc in range(2)]
    owner = jnp.stack([2 * ((x - dx) % nx) + (c - dc) % 2 for dx, dc in places]).astype(jnp.int32)
    inverse = jnp.stack(
        [2 * ((x - j // 2) % nx) + (c - j % 2) % 2 for j in range(ng)]
    ).astype(jnp.int32)

    w3 = jnp.stack([w_query, w_key, w_value], axis=1).reshape(-1, 3, ng, cols)
    w3 = w3.transpose(2, 0, 1, 3).reshape(ng, -1, 3 * cols)
    w3 = lax.all_to_all(w3, GROUP, split_axis=0, concat_axis=0, tiled=True)
    w3 = lax.all_gather(w3.reshape(-1, 3 * cols), ("r", "y"), axis=0, tiled=True)
    extras = jnp.concatenate(
        [w_router, attn_gain[:, None], query_gain[:, None], key_gain[:, None], ffn_gain[:, None]], axis=1
    )
    extras = lax.all_gather(extras, ALL, axis=0, tiled=True)
    out_full = lax.all_gather(w_out, ALL, axis=0, tiled=True)
    router_full = extras[:, :EXPERTS]
    attn_g, query_g, key_g, ffn_g = (extras[:, EXPERTS + i].astype(F32) for i in range(4))
    query_g = lax.dynamic_slice(query_g, (me * cols,), (cols,))
    key_g = lax.dynamic_slice(key_g, (me * cols,), (cols,))

    choose = routes.reshape(token_count, top_count)
    chosen = jnp.sum(
        (choose[:, :, None] == jnp.arange(EXPERTS, dtype=jnp.int32)).astype(F32), axis=1
    )
    tri = (
        lax.broadcasted_iota(jnp.int32, (token_count, token_count), 0)
        > lax.broadcasted_iota(jnp.int32, (token_count, token_count), 1)
    ).astype(BF)
    rank = jnp.where(chosen > 0, dot(tri, chosen.astype(BF)), -1.0)

    def gather_group(value):
        pieces = []
        for dx in range(nx):
            far = shift(value, "x", dx) if dx else value
            pieces += [far, shift(far, "c", 1)]
        return pieces

    own_places = me * span + jnp.arange(span, dtype=jnp.int32)
    valid = (own_places[None, :] < lengths[:, None]).reshape(token_count)
    own_cot = jnp.where(valid[:, None], cotangent.reshape(token_count, width), jnp.zeros((), BF))
    own_tokens = tokens.astype(F32).reshape(token_count, width)

    all_tokens = jnp.stack(gather_group(tokens)).reshape(ng * token_count, width).astype(F32)
    normed_n = rms_parts(all_tokens)
    normed = (normed_n * attn_g).astype(BF)

    def sum_group(stats):
        stats = stats.reshape(2, ng, token_count)
        stats = jnp.concatenate([lax.dynamic_slice_in_dim(stats, inverse[j], 1, 1) for j in range(ng)], 1)
        stats = lax.psum(stats, GROUP)
        stats = jnp.concatenate([lax.dynamic_slice_in_dim(stats, owner[p], 1, 1) for p in range(ng)], 1)
        return stats.reshape(2, ng * token_count)

    raw = dot(normed, w3)
    query_raw, key_raw = raw[:, :cols], raw[:, cols : 2 * cols]
    value = raw[:, 2 * cols :].astype(BF)
    squares = jnp.stack([jnp.sum(query_raw * query_raw, -1), jnp.sum(key_raw * key_raw, -1)])
    squares = sum_group(squares)
    factor = lax.rsqrt(squares / width + EPS)

    half = HEAD_DIM // 2
    frequencies = jnp.exp(jnp.arange(half, dtype=F32) * (-2.0 * math.log(10000.0) / HEAD_DIM))
    spot = owner[:, None] * span + jnp.arange(span, dtype=jnp.int32)[None, :]
    angles = spot.astype(F32)[:, :, None] * frequencies
    cosine, sine = jnp.cos(angles), jnp.sin(angles)
    cosine = jnp.concatenate([cosine, cosine], -1)[:, None, :, None, :]
    sine = jnp.concatenate([-sine, sine], -1)[:, None, :, None, :]

    def turn(v, sign):
        v = v.reshape(ng, seqs, span, -1, HEAD_DIM)
        swapped = jnp.concatenate([v[..., half:], v[..., :half]], -1)
        return (v * cosine + sign * swapped * sine).reshape(ng * token_count, cols)

    blocked = (ng, seqs, span, cols)
    query_n = query_raw * factor[0][:, None]
    key_n = key_raw * factor[1][:, None]
    query = turn(query_n * query_g, 1.0).astype(BF).reshape(blocked)
    key = turn(key_n * key_g, 1.0).astype(BF).reshape(blocked)
    value = value.reshape(blocked)
    pair_flops = 2 * length * length * seqs * cols * 5 // 8
    (attended,) = attention_call(
        attend_kernel, inverse, lengths, [query, key, value], [BF], [], 2 * pair_flops
    )
    attended = lax.all_to_all(attended, GROUP, split_axis=0, concat_axis=0, tiled=True)
    attended = attended.reshape(ng, token_count, cols).transpose(1, 0, 2).reshape(token_count, width)
    resid = own_tokens + dot(attended, out_full)
    ffn_scale = lax.rsqrt(jnp.mean(resid * resid, axis=-1, keepdims=True) + EPS)
    ffn_n = resid * ffn_scale
    ffn_in = (ffn_n * ffn_g).astype(BF)
    logits = dot(ffn_in, router_full)
    router = jnp.exp(logits - jnp.max(logits, axis=-1, keepdims=True))
    router = router / jnp.sum(router, axis=-1, keepdims=True)

    spots = [(dy, dx) for dy in range(2) for dx in range(nx)]

    def gather_pair(value):
        out = {(0, 0): value}
        for dx in range(1, nx):
            out[0, dx] = shift(value, "x", dx)
        for dx in range(nx):
            out[1, dx] = shift(out[0, dx], "y", 1)
        return {(dy, dx, dc): shift(v, "c", 1) if dc else v for (dy, dx), v in out.items() for dc in range(2)}

    def gather_pair_late(value):
        out = {(0, 0): value, (1, 0): shift(value, "y", 1)}
        for dx in range(1, nx):
            out[0, dx] = shift(value, "x", dx)
            out[1, dx] = shift(out[1, 0], "x", dx)
        return {(dy, dx, dc): shift(v, "c", 1) if dc else v for (dy, dx), v in out.items() for dc in range(2)}

    def gather_halves(value):
        h = token_count // 2
        return gather_pair(value[:h]), gather_pair_late(value[h:])

    cots = gather_halves(own_cot)
    ranks = gather_pair(rank)
    ranks_t = gather_pair(rank.T)
    gates_t = gather_pair(router.T)
    feats = gather_halves(ffn_in)

    local_experts = w_gate.shape[0]
    mine = local_experts // 2
    base = jnp.stack([y * mine, me * local_experts + y * mine]).astype(jnp.int32)
    before, gate_terms = None, {}
    for g, (dy, dx) in enumerate(spots):
        both = lambda halves: [halves[h][dy, dx, dc] for dc in range(2) for h in range(2)]
        pair = lambda table: [table[dy, dx, dc] for dc in range(2)]
        *before, gg = experts_in(
            g, len(spots), base, both(feats), both(cots), pair(ranks_t), pair(gates_t), w_gate, w_up, w_down, cap, mine, before
        )
        gate_terms[dy, dx] = gg
    buf, og, hg, dg, du = before

    def weight_grad(left, right):
        full = lax.dot_general(
            left, right, (((1,), (1,)), ((0,), (0,))), preferred_element_type=F32
        ).astype(BF)
        return lax.psum_scatter(full, "r", scatter_dimension=1, tiled=True)

    def finish_grad(part):
        rows = part.shape[1] // 2
        keep = lax.dynamic_slice_in_dim(part, y * rows, rows, 1)
        give = shift(lax.dynamic_slice_in_dim(part, (1 - y) * rows, rows, 1), "y", 1)
        first = jnp.where(y == 0, keep, give)
        second = jnp.where(y == 0, give, keep)
        return jnp.concatenate([first, second], axis=0).astype(F32)

    grad_down = finish_grad(weight_grad(og, hg)).transpose(0, 2, 1)
    grad_gate = finish_grad(weight_grad(buf, dg))
    grad_up = finish_grad(weight_grad(buf, du))

    mixes, backs = {}, {}
    for g, (dy, dx) in reversed(list(enumerate(spots))):
        m0, m1, d0, d1 = experts_out(
            g, base, hg, dg, du, [ranks[dy, dx, dc] for dc in range(2)], w_gate, w_up, w_down, cap, mine
        )
        mixes[dy, dx] = (m0, m1)
        backs[dy, dx] = (d0, d1)

    def send_back(parts):
        acc = {k: add_low(p0, shift(p1, "c", 1)) for k, (p0, p1) in parts.items()}
        h = token_count // 2
        top = {k: v[:h] for k, v in acc.items()}
        low = {k: v[h:] for k, v in acc.items()}
        far = add_low(top[1, 0], *[shift(top[1, dx], "x", -dx) for dx in range(1, nx)])
        top = [top[0, 0], shift(far, "y", 1)] + [shift(top[0, dx], "x", -dx) for dx in range(1, nx)]
        near = [low[0, 0], shift(low[1, 0], "y", 1)]
        for dx in range(1, nx):
            near.append(shift(add_low(low[0, dx], shift(low[1, dx], "y", 1)), "x", -dx))
        total = lambda terms: sum(t.astype(F32) for t in terms)
        return jnp.concatenate([total(top), total(near)], axis=0)

    dffn = send_back(backs)
    mixture = send_back(mixes)
    output = (resid + mixture).astype(BF).reshape(seqs, span, width)

    terms = jnp.stack([gate_terms[k] for k in spots])
    terms = terms.reshape(2, nx, mine, 2, token_count)
    order = []
    for k in range(2 * ng):
        ty, tx, tc = k // ng, (k % ng) // 2, k % 2
        piece = lax.dynamic_slice(
            terms, ((y - ty) % 2, (x - tx) % nx, 0, (c - tc) % 2, 0), (1, 1, mine, 1, token_count)
        )
        order.append(piece.reshape(mine, token_count))
    terms = lax.all_to_all(jnp.stack(order), ("y", "x", "c"), split_axis=0, concat_axis=0, tiled=True)
    drouter = terms.reshape(2, ng, mine, token_count).transpose(1, 0, 2, 3).reshape(EXPERTS, token_count).T

    dlogits = router * (drouter - jnp.sum(router * drouter, axis=-1, keepdims=True))
    highest = lax.Precision.HIGHEST
    grad_router = lax.dot_general(ffn_in.astype(F32), dlogits, (((0,), (0,)), ((), ())), precision=highest)
    dffn = dffn + lax.dot_general(
        dlogits, router_full.astype(F32), (((1,), (1,)), ((), ())), precision=highest
    )
    grad_ffn_g = jnp.sum(dffn * ffn_n, axis=0)
    gd = dffn * ffn_g
    dresid = own_cot.astype(F32) + ffn_scale * (gd - ffn_n * jnp.mean(gd * ffn_n, axis=-1, keepdims=True))

    dattn = dresid.astype(BF)
    grad_out = dot(attended, dattn, TN).astype(BF)
    dattended = dot(dattn, out_full, NT).astype(BF)
    dattended = dattended.reshape(token_count, ng, cols).transpose(1, 0, 2).reshape(blocked)
    dattended = lax.all_to_all(dattended, GROUP, split_axis=0, concat_axis=0, tiled=True)
    dquery, dkey, dvalue = attention_call(
        attend_back_kernel,
        inverse,
        lengths,
        [query, key, value, dattended],
        [F32, F32, BF],
        [pltpu.VMEM((ng, span, HEAD_DIM), F32)] * 2,
        5 * pair_flops,
    )
    dquery = turn(dquery.reshape(-1, cols), -1.0)
    dkey = turn(dkey.reshape(-1, cols), -1.0)
    means = jnp.stack(
        [jnp.sum(dquery * query_g * query_n, -1), jnp.sum(dkey * key_g * key_n, -1)]
    )
    means = sum_group(means) / width
    dquery_raw = factor[0][:, None] * (dquery * query_g - query_n * means[0][:, None])
    dkey_raw = factor[1][:, None] * (dkey * key_g - key_n * means[1][:, None])
    grad_query_g = jnp.sum(dquery * query_n, axis=0)
    grad_key_g = jnp.sum(dkey * key_n, axis=0)
    draw = jnp.concatenate(
        [dquery_raw.astype(BF), dkey_raw.astype(BF), dvalue.reshape(-1, cols)], axis=1
    )
    grad_three = dot(normed, draw, TN).astype(BF)
    dnormed = dot(draw, w3, NT)
    grad_attn_g = jnp.sum(dnormed * normed_n, axis=0)
    dnormed = dnormed.astype(BF).reshape(nx, 2, token_count, width)
    dnormed = [add_low(dnormed[dx, 0], shift(dnormed[dx, 1], "c", 1)) for dx in range(nx)]
    dnormed = sum(
        (shift(dnormed[dx], "x", -dx) if dx else dnormed[0]).astype(F32) for dx in range(nx)
    )
    own_scale = lax.rsqrt(jnp.mean(own_tokens * own_tokens, axis=-1, keepdims=True) + EPS)
    own_n = own_tokens * own_scale
    gd = dnormed * attn_g
    grad_input = dresid + own_scale * (gd - own_n * jnp.mean(gd * own_n, axis=-1, keepdims=True))
    grad_input = grad_input.reshape(seqs, span, width)

    def swap_y(part):
        keep = lax.dynamic_index_in_dim(part, y, 1, keepdims=False)
        give = lax.dynamic_index_in_dim(part, 1 - y, 1, keepdims=False)
        return add_low(keep, shift(give, "y", 1))

    g3 = swap_y(grad_three.reshape(nr, 2, -1, 3 * cols))
    g3 = lax.psum_scatter(g3, "r", scatter_dimension=0, tiled=True)
    g3 = lax.all_to_all(g3.reshape(ng, -1, 3 * cols), GROUP, split_axis=0, concat_axis=0, tiled=True)
    rows = g3.shape[1]
    g3 = g3.reshape(ng, rows, 3, cols).transpose(2, 1, 0, 3).reshape(3, rows, width).astype(F32)

    go = grad_out.reshape(nr * 2, nx, 2, rows, width)
    keep = lax.dynamic_index_in_dim(go, c, 2, keepdims=False)
    give = lax.dynamic_index_in_dim(go, 1 - c, 2, keepdims=False)
    go = add_low(keep, shift(give, "c", 1))
    go = add_low(
        *[
            shift(lax.dynamic_index_in_dim(go, (x + dx) % nx, 1, keepdims=False), "x", dx)
            if dx
            else lax.dynamic_index_in_dim(go, x, 1, keepdims=False)
            for dx in range(nx)
        ]
    )
    go = swap_y(go.reshape(nr, 2, rows, width))
    go = lax.psum_scatter(go, "r", scatter_dimension=0, tiled=True).reshape(rows, width).astype(F32)

    spread = lambda v: lax.dynamic_update_slice(jnp.zeros((width,), F32), v, (me * cols,))
    sums = jnp.concatenate(
        [
            grad_router,
            grad_attn_g[:, None],
            spread(grad_query_g)[:, None],
            spread(grad_key_g)[:, None],
            grad_ffn_g[:, None],
        ],
        axis=1,
    )
    sums = lax.psum_scatter(sums, ALL, scatter_dimension=0, tiled=True)
    return (
        output,
        grad_input,
        g3[0],
        g3[1],
        g3[2],
        go,
        sums[:, :EXPERTS],
        sums[:, EXPERTS],
        sums[:, EXPERTS + 1],
        sums[:, EXPERTS + 2],
        sums[:, EXPERTS + 3],
        grad_gate,
        grad_up,
        grad_down,
    )


def solution(mesh):
    ndp, nex = mesh.shape["dp"], mesh.shape["expert"]
    nx = nex // 2
    fine = Mesh(mesh.devices.reshape(ndp // 2, 2, nx, 2), ("r", "y", "x", "c"))
    dp, ex = ("r", "y"), ("x", "c")
    both = dp + ex
    placed = (
        P(dp, ex, None),
        P(dp),
        P(dp, ex, None, None),
        P(both, None),
        P(both, None),
        P(both, None),
        P(both, None),
        P(both, None),
        P(both),
        P(both),
        P(both),
        P(both),
        P(ex, None, None),
        P(ex, None, None),
        P(ex, None, None),
        P(dp, ex, None),
    )
    return jax.shard_map(
        partial(local, nx),
        mesh=fine,
        in_specs=placed,
        out_specs=(
            P(dp, ex, None),
            P(dp, ex, None),
            P(both, None),
            P(both, None),
            P(both, None),
            P(both, None),
            P(both, None),
            P(both),
            P(both),
            P(both),
            P(both),
            P(ex, dp, None),
            P(ex, dp, None),
            P(ex, None, dp),
        ),
        check_vma=False,
    )
```

```python
from functools import partial
import math

import jax
import jax.numpy as jnp
from jax import lax
from jax.experimental import pallas as pl
from jax.experimental.pallas import tpu as pltpu
from jax.sharding import Mesh, PartitionSpec as P

HEAD_DIM = 128
EXPERTS = 16
EPS = 1e-05
F32 = jnp.float32
BF = jnp.bfloat16
VMEM_LIMIT = 60 * 1024 * 1024


def dot(a, b, dims=((1,), (0,))):
    return lax.dot_general(a, b, (dims, ((), ())), preferred_element_type=F32)


NT = ((1,), (1,))
TN = ((0,), (0,))


def masked_scores(q, k, i, j, rows, length, scale):
    s = dot(q, k, NT) * scale
    col = j * rows + lax.broadcasted_iota(jnp.int32, s.shape, 1)
    ok = col < length
    if i == j:
        row = i * rows + lax.broadcasted_iota(jnp.int32, s.shape, 0)
        ok = ok & (col <= row)
    return jnp.where(ok, s, -1e30)


def probs_of(q, key, i, rows, length, scale):
    parts = [masked_scores(q, key[j], i, j, rows, length, scale) for j in range(i + 1)]
    peak = parts[0].max(axis=1, keepdims=True)
    for s in parts[1:]:
        peak = jnp.maximum(peak, s.max(axis=1, keepdims=True))
    parts = [jnp.exp(s - peak) for s in parts]
    total = parts[0].sum(axis=1, keepdims=True)
    for e in parts[1:]:
        total = total + e.sum(axis=1, keepdims=True)
    inverse = 1.0 / total
    return [e * inverse for e in parts]


def turned(v, cosine, sine):
    return v * cosine + pltpu.roll(v, HEAD_DIM // 2, 1) * sine


def normed_turned(raw, factor, gain, cosine, sine):
    return turned(raw * factor * gain, cosine, sine).astype(BF)


def attend_kernel(inv, lens, q_ref, k_ref, v_ref, fac_ref, qg_ref, kg_ref, cos_ref, sin_ref, o_ref, key, *, first, blocks, rows, scale):
    length = lens[first + pl.program_id(0)]
    for i in range(blocks):
        at = inv[i]
        fac, cosine, sine = fac_ref[at], cos_ref[at], sin_ref[at]
        q = normed_turned(q_ref[at], fac[:, 0:1], qg_ref[...], cosine, sine)
        key[i] = normed_turned(k_ref[at], fac[:, 1:2], kg_ref[...], cosine, sine)
        probs = probs_of(q, key, i, rows, length, scale)
        out = jnp.zeros((rows, HEAD_DIM), F32)
        for j, p in enumerate(probs):
            out = out + dot(p.astype(BF), v_ref[inv[j]].astype(BF))
        o_ref[i] = out.astype(BF)


def attend_back_kernel(
    inv, lens, q_ref, k_ref, v_ref, fac_ref, qg_ref, kg_ref, cos_ref, sin_ref, do_ref,
    dq_ref, dk_ref, dv_ref, stat_ref, gain_ref, key, dk_acc, dv_acc, *, first, blocks, rows, scale
):
    length = lens[first + pl.program_id(0)]
    head = pl.program_id(1)
    dk_acc[...] = jnp.zeros_like(dk_acc)
    dv_acc[...] = jnp.zeros_like(dv_acc)

    @pl.when(head == 0)
    def _():
        stat_ref[...] = jnp.zeros_like(stat_ref)

    def unturn(at, grad, raw_ref, which, gain, out_ref):
        grad = turned(grad * scale, cos_ref[at], -sin_ref[at])
        out_ref[at] = grad
        weighted = grad * (raw_ref[at] * fac_ref[at][:, which : which + 1])
        stat_ref[at, :, which : which + 1] += jnp.sum(weighted * gain, axis=1, keepdims=True)
        return jnp.sum(weighted, axis=0, keepdims=True)

    qg, kg = qg_ref[...], kg_ref[...]
    dqg = jnp.zeros((1, HEAD_DIM), F32)
    dkg = jnp.zeros((1, HEAD_DIM), F32)
    for i in range(blocks):
        at = inv[i]
        fac, cosine, sine = fac_ref[at], cos_ref[at], sin_ref[at]
        q = normed_turned(q_ref[at], fac[:, 0:1], qg, cosine, sine)
        key[i] = normed_turned(k_ref[at], fac[:, 1:2], kg, cosine, sine)
        do = do_ref[i]
        probs = probs_of(q, key, i, rows, length, scale)
        dprobs = [dot(do, v_ref[inv[j]].astype(BF), NT) for j in range(i + 1)]
        delta = jnp.zeros((rows, 1), F32)
        for p, dp in zip(probs, dprobs):
            delta = delta + jnp.sum(p * dp, axis=1, keepdims=True)
        dq = jnp.zeros((rows, HEAD_DIM), F32)
        for j, (p, dp) in enumerate(zip(probs, dprobs)):
            ds = (p * (dp - delta)).astype(BF)
            dq = dq + dot(ds, key[j])
            dk_acc[j] += dot(ds, q, TN)
            dv_acc[j] += dot(p.astype(BF), do, TN)
        dqg = dqg + unturn(at, dq, q_ref, 0, qg, dq_ref)
    for j in range(blocks):
        at = inv[j]
        dkg = dkg + unturn(at, dk_acc[j], k_ref, 1, kg, dk_ref)
        dv_ref[at] = dv_acc[j].astype(BF)
    gain_ref[0:1, :] = dqg
    gain_ref[1:2, :] = dkg


def attention_call(lens, raw, factor, query_g, key_g, cosine, sine, first, seqs, inverse, grad=None):
    blocks, _, rows, width = raw.shape
    heads = width // (3 * HEAD_DIM)
    part = lambda k: pl.BlockSpec((blocks, None, rows, HEAD_DIM), lambda s, h, *_: (0, first + s, 0, k * heads + h))
    out = pl.BlockSpec((blocks, None, rows, HEAD_DIM), lambda s, h, *_: (0, s, 0, h))
    fac = pl.BlockSpec((blocks, None, rows, 2), lambda s, h, *_: (0, first + s, 0, 0))
    gain = pl.BlockSpec((1, HEAD_DIM), lambda s, h, *_: (0, h))
    turn = pl.BlockSpec((blocks, rows, HEAD_DIM), lambda s, h, *_: (0, 0, 0))
    ins = [raw, raw, raw, factor, query_g, key_g, cosine, sine]
    in_specs = [part(0), part(1), part(2), fac, gain, gain, turn, turn]
    one = (blocks, seqs, rows, width // 3)
    shape = jax.ShapeDtypeStruct
    scratch = [pltpu.VMEM((blocks, rows, HEAD_DIM), BF)]
    flops = 2 * 2 * (blocks * rows) ** 2 * seqs * width // 3 * 5 // 8
    if grad is None:
        kernel, outs, out_specs = attend_kernel, [shape(one, BF)], [out]
    else:
        ins, in_specs = ins + [grad], in_specs + [out]
        kernel = attend_back_kernel
        outs = [shape(one, F32), shape(one, F32), shape(one, BF)]
        outs += [shape((blocks, seqs, rows, 2), F32), shape((seqs, 2, width // 3), F32)]
        out_specs = [out] * 3 + [fac, pl.BlockSpec((None, 2, HEAD_DIM), lambda s, h, *_: (s, 0, h))]
        scratch += [pltpu.VMEM((blocks, rows, HEAD_DIM), F32)] * 2
        flops = flops * 5 // 2
    return pl.pallas_call(
        partial(kernel, first=first, blocks=blocks, rows=rows, scale=1.0 / math.sqrt(HEAD_DIM)),
        out_shape=outs,
        grid_spec=pltpu.PrefetchScalarGridSpec(
            num_scalar_prefetch=2, grid=(seqs, heads), in_specs=in_specs, out_specs=out_specs, scratch_shapes=scratch
        ),
        compiler_params=pltpu.CompilerParams(vmem_limit_bytes=VMEM_LIMIT),
        cost_estimate=pl.CostEstimate(
            flops=flops, bytes_accessed=raw.size * 6, transcendentals=(blocks * rows) ** 2 * seqs * heads * 5 // 8
        ),
    )(inverse, lens, *ins)


def pick_row(table, index):
    which = lax.broadcasted_iota(jnp.int32, table.shape, 0) == index
    return jnp.sum(jnp.where(which, table, 0.0), axis=0, keepdims=True)


def selection(rank_table, expert, cap):
    rank = pick_row(rank_table, expert)
    return lax.broadcasted_iota(jnp.int32, (cap, rank.shape[1]), 0).astype(F32) == rank


def dispatch(out, b, s, top, low, cap):
    half = top.shape[0]
    s = s.astype(F32).astype(BF)
    out[pl.ds(b * cap, cap), :] = (dot(s[:, :half], top[...]) + dot(s[:, half:], low[...])).astype(BF)


def experts_grad_kernel(base, c00, c01, c10, c11, r0, r1, wd, *rest, cap):
    og, dh = rest[-2:]
    expert = base[1] + pl.program_id(0)

    @pl.when(pl.program_id(1) == 0)
    def _():
        for b, (r, top, low) in enumerate(((r0, c00, c01), (r1, c10, c11))):
            dispatch(og, b, selection(r[...], expert, cap), top, low, cap)

    dh[...] = dot(og[...], wd[...], NT)


def experts_in_kernel(base, f00, f01, f10, f11, r0, r1, g0, g1, dhu, wg, wu, *rest, cap):
    buf, hg, dg, du, gg, weight, dots = rest[-7:]
    f = pl.program_id(1)
    expert = base[1] + pl.program_id(0)

    @pl.when(f == 0)
    def _():
        for b, (r, g, top, low) in enumerate(((r0, g0, f00, f01), (r1, g1, f10, f11))):
            s = selection(r[...], expert, cap)
            dispatch(buf, b, s, top, low, cap)
            gate = pick_row(g[...], expert)
            weight[pl.ds(b * cap, cap), :] = jnp.sum(jnp.where(s, gate, 0.0), axis=1, keepdims=True)
        dots[...] = jnp.zeros_like(dots)

    x = buf[...]
    gate = dot(x, wg[...])
    up = dot(x, wu[...])
    dh = dhu[...]
    w = weight[...]
    sg = 1.0 / (1.0 + jnp.exp(-gate))
    silu = gate * sg
    hidden = (silu * up).astype(BF).astype(F32)
    dots[...] += jnp.sum(hidden * dh, axis=1, keepdims=True)
    dh = dh * w
    hg[...] = (hidden * w).astype(BF)
    dg[...] = (dh * up * (sg * (1.0 + gate * (1.0 - sg)))).astype(BF)
    du[...] = (dh * silu).astype(BF)

    @pl.when(f == pl.num_programs(1) - 1)
    def _():
        for b, r in enumerate((r0, r1)):
            s = selection(r[...], expert, cap)
            gg[b] = jnp.sum(jnp.where(s, dots[pl.ds(b * cap, cap), :], 0.0), axis=0, keepdims=True)


def experts_call(kernel, group, groups, base, small, wide_ins, weights, wide_outs, gates, cap, local, before, flops):
    tile = 512
    width = weights[-1].shape[1] if gates else weights[-1].shape[2]
    ff = weights[-1].shape[2] if gates else weights[-1].shape[1]
    rows = 2 * cap
    tokens = small[0].shape[0] * 2
    whole = lambda a: pl.BlockSpec(a.shape, lambda e, f, s: (0, 0), pipeline_mode=pl.Buffered(1))
    wide = pl.BlockSpec((None, rows, width), lambda e, f, s: (e, group, 0))
    thin = pl.BlockSpec((None, rows, tile), lambda e, f, s: (e, group, f))
    if gates:
        heavy = pl.BlockSpec((None, width, tile), lambda e, f, s: (s[0] + e, 0, f))
    else:
        heavy = pl.BlockSpec((None, tile, width), lambda e, f, s: (s[0] + e, f, 0))
    shape = jax.ShapeDtypeStruct
    outs = [shape((local, groups * rows, width if w else ff), t) for w, t in wide_outs]
    out_specs = [wide if w else thin for w, _ in wide_outs]
    scratch = []
    if gates:
        outs.append(shape((local, 2, 1, tokens), F32))
        out_specs.append(pl.BlockSpec((None, 2, 1, tokens), lambda e, f, s: (e, 0, 0, 0)))
        scratch = [pltpu.VMEM((rows, 1), F32)] * 2
    before = [] if before is None else before
    n = 1 + len(small) + len(wide_ins) + len(weights)
    return pl.pallas_call(
        partial(kernel, cap=cap),
        out_shape=outs,
        grid_spec=pltpu.PrefetchScalarGridSpec(
            num_scalar_prefetch=1,
            grid=(local, ff // tile),
            in_specs=[whole(a) for a in small]
            + [thin] * len(wide_ins)
            + [heavy] * len(weights)
            + [pl.BlockSpec(memory_space=pl.ANY)] * len(before),
            out_specs=out_specs,
            scratch_shapes=scratch,
        ),
        input_output_aliases={n + i: i for i in range(len(before))},
        compiler_params=pltpu.CompilerParams(vmem_limit_bytes=VMEM_LIMIT),
        cost_estimate=pl.CostEstimate(
            flops=flops,
            bytes_accessed=local * (len(weights) * width * ff * 2 + rows * (2 * width + 10 * ff)) + 4 * tokens * width,
            transcendentals=local * rows * ff if gates else 0,
        ),
    )(base, *small, *wide_ins, *weights, *before)


def experts_grad(group, groups, base, cots, ranks, wd, cap, local, before):
    flops = local * 2 * cap * wd.shape[2] * (2 * wd.shape[1] + 4 * cots[0].shape[0])
    return experts_call(
        experts_grad_kernel, group, groups, base, [*cots, *ranks], [], [wd], [(True, BF), (False, F32)],
        False, cap, local, before, flops,
    )


def experts_in(group, groups, base, feats, ranks, gates, dhu, wg, wu, cap, local, before):
    flops = local * 2 * cap * wg.shape[1] * (4 * wg.shape[2] + 4 * feats[0].shape[0])
    return experts_call(
        experts_in_kernel, group, groups, base, [*feats, *ranks, *gates], [dhu], [wg, wu],
        [(True, BF), (False, BF), (False, BF), (False, BF)], True, cap, local, before, flops,
    )


def experts_out_kernel(base, *refs, cap, forward):
    if forward:
        hg, r0, r1, wd, t0, t1 = refs
        parts = [dot(hg[e], wd[e]).astype(BF) for e in range(hg.shape[0])]
    else:
        dg, du, r0, r1, wg, wu, t0, t1 = refs
        parts = [(dot(dg[e], wg[e], NT) + dot(du[e], wu[e], NT)).astype(BF) for e in range(dg.shape[0])]
    for b, (rank, final) in enumerate(((r0, t0), (r1, t1))):
        table = rank[...]
        total = None
        for e, part in enumerate(parts):
            which = lax.broadcasted_iota(jnp.int32, table.shape, 1) == base[1] + e
            column = jnp.sum(jnp.where(which, table, 0.0), axis=1, keepdims=True)
            slot = lax.broadcasted_iota(jnp.int32, (table.shape[0], cap), 1).astype(F32)
            pick = (slot == column).astype(F32).astype(BF)
            term = dot(pick, part[b * cap : (b + 1) * cap])
            total = term if total is None else total + term
        final[...] = total.astype(BF)


def experts_out(group, base, rows_in, ranks, weights, cap, local, forward):
    tokens = ranks[0].shape[0]
    width, ff = weights[0].shape[1:]
    if forward:
        ff, width = width, ff
    tile = 512
    rows = 2 * cap
    thin = pl.BlockSpec((local, rows, ff), lambda d, s: (0, group, 0))
    whole = pl.BlockSpec((tokens, EXPERTS), lambda d, s: (0, 0))
    final = pl.BlockSpec((tokens, tile), lambda d, s: (0, d))
    if forward:
        heavy = pl.BlockSpec((local, ff, tile), lambda d, s: (s[2], 0, d))
    else:
        heavy = pl.BlockSpec((local, tile, ff), lambda d, s: (s[2], d, 0))
    n = len(weights)
    return pl.pallas_call(
        partial(experts_out_kernel, cap=cap, forward=forward),
        out_shape=[jax.ShapeDtypeStruct((tokens, width), BF)] * 2,
        grid_spec=pltpu.PrefetchScalarGridSpec(
            num_scalar_prefetch=1,
            grid=(width // tile,),
            in_specs=[thin] * n + [whole] * 2 + [heavy] * n,
            out_specs=[final] * 2,
        ),
        compiler_params=pltpu.CompilerParams(vmem_limit_bytes=VMEM_LIMIT),
        cost_estimate=pl.CostEstimate(
            flops=local * rows * width * (2 * n * ff + 2 * tokens),
            bytes_accessed=local * n * (width * ff + rows * ff) * 2 + 4 * tokens * width,
            transcendentals=0,
        ),
    )(base, *rows_in, *ranks, *weights)


def shift(value, axis, by):
    n = lax.axis_size(axis)
    return lax.ppermute(value, axis, [(i, (i + by) % n) for i in range(n)])


def gather_small(value, axis):
    n, index, rows = lax.axis_size(axis), lax.axis_index(axis), value.shape[0]
    out = jnp.zeros((n * rows, *value.shape[1:]), value.dtype)
    for by in range(n):
        piece = shift(value, axis, by) if by else value
        out = lax.dynamic_update_slice_in_dim(out, piece, (index - by) % n * rows, 0)
    return out


def scatter_small(value, axis):
    n, index = lax.axis_size(axis), lax.axis_index(axis)
    value = value.reshape(n, -1, *value.shape[1:])
    part = lambda i: lax.dynamic_index_in_dim(value, i % n, 0, keepdims=False)
    total = part(index)
    for by in range(1, n):
        total = total + shift(part(index + by), axis, by)
    return total


def tie(*values):
    return lax.optimization_barrier(values)


def add_low(*terms):
    total = terms[0].astype(F32)
    for t in terms[1:]:
        total = total + t.astype(F32)
    return total.astype(BF)


def rms_parts(values):
    return values * lax.rsqrt(jnp.mean(values * values, axis=-1, keepdims=True) + EPS)


def local(
    nx,
    tokens,
    lengths,
    routes,
    w_query,
    w_key,
    w_value,
    w_out,
    w_router,
    attn_gain,
    query_gain,
    key_gain,
    ffn_gain,
    w_gate,
    w_up,
    w_down,
    cotangent,
):
    ALL, GROUP = ("r", "y", "x", "c"), ("x", "c")
    r, y, x, c = (lax.axis_index(a) for a in ALL)
    nr = lax.axis_size("r")
    me = 2 * x + c
    ng = 2 * nx
    seqs, span, width = tokens.shape
    token_count = seqs * span
    top_count = routes.shape[-1]
    cap = (token_count * top_count * 9 + 8 * EXPERTS - 1) // (8 * EXPERTS)
    cols = width // ng
    length = span * ng
    places = [(dx, dc) for dx in range(nx) for dc in range(2)]
    owner = jnp.stack([2 * ((x - dx) % nx) + (c - dc) % 2 for dx, dc in places]).astype(jnp.int32)
    inverse = jnp.stack(
        [2 * ((x - j // 2) % nx) + (c - j % 2) % 2 for j in range(ng)]
    ).astype(jnp.int32)

    w3 = jnp.stack([w_query, w_key, w_value], axis=1).reshape(-1, 3, ng, cols)
    w3 = w3.transpose(2, 0, 1, 3).reshape(ng, -1, 3 * cols)
    w3 = lax.all_to_all(w3, GROUP, split_axis=0, concat_axis=0, tiled=True)
    w3 = lax.all_gather(w3.reshape(-1, 3 * cols), ("r", "y"), axis=0, tiled=True)
    extras = jnp.concatenate(
        [w_router, attn_gain[:, None], query_gain[:, None], key_gain[:, None], ffn_gain[:, None]], axis=1
    )
    for axis in reversed(ALL):
        extras = gather_small(extras, axis)
    out_full = lax.all_gather(w_out, ALL, axis=0, tiled=True)
    router_full = extras[:, :EXPERTS]
    attn_g, query_g, key_g, ffn_g = (extras[:, EXPERTS + i].astype(F32) for i in range(4))
    query_g = lax.dynamic_slice(query_g, (me * cols,), (cols,))
    key_g = lax.dynamic_slice(key_g, (me * cols,), (cols,))

    choose = routes.reshape(token_count, top_count)
    chosen = jnp.sum(
        (choose[:, :, None] == jnp.arange(EXPERTS, dtype=jnp.int32)).astype(F32), axis=1
    )
    tri = (
        lax.broadcasted_iota(jnp.int32, (token_count, token_count), 0)
        > lax.broadcasted_iota(jnp.int32, (token_count, token_count), 1)
    ).astype(BF)
    rank = jnp.where(chosen > 0, dot(tri, chosen.astype(BF)), -1.0)

    def gather_group(value):
        pieces = []
        for dx in range(nx):
            far = shift(value, "x", dx) if dx else value
            pieces += [far, shift(far, "c", 1)]
        return pieces

    own_places = me * span + jnp.arange(span, dtype=jnp.int32)
    valid = (own_places[None, :] < lengths[:, None]).reshape(token_count)
    own_cot = jnp.where(valid[:, None], cotangent.reshape(token_count, width), jnp.zeros((), BF))
    own_tokens = tokens.astype(F32).reshape(token_count, width)

    all_tokens = jnp.stack(gather_group(tokens)).reshape(ng * token_count, width).astype(F32)
    h = token_count // 2
    cot_halves = [own_cot[:h], own_cot[h:]]
    near = [{dx: shift(v, "x", dx) if dx else v for dx in range(nx)} for v in cot_halves]
    normed_n = rms_parts(all_tokens)
    normed = (normed_n * attn_g).astype(BF)

    spots = [(dy, dx) for dy in range(2) for dx in range(nx)]

    def gather_pair(value):
        out = {(0, 0): value}
        for dx in range(1, nx):
            out[0, dx] = shift(value, "x", dx)
        for dx in range(nx):
            out[1, dx] = shift(out[0, dx], "y", 1)
        return {(dy, dx, dc): shift(v, "c", 1) if dc else v for (dy, dx), v in out.items() for dc in range(2)}

    def with_core(pieces):
        return pieces | {(dy, dx, 1): shift(v, "c", 1) for (dy, dx, _), v in pieces.items()}

    ranks_t = gather_pair(rank.T)
    ranks = {k: v.T for k, v in ranks_t.items()}
    w3, normed, ranks_t = lax.optimization_barrier((w3, normed, ranks_t))

    local_experts = w_gate.shape[0]
    mine = local_experts // 2
    base = jnp.stack([y * mine, me * local_experts + y * mine, y]).astype(jnp.int32)
    both = lambda halves, dy, dx: [halves[h][dy, dx, dc] for dc in range(2) for h in range(2)]
    pair = lambda table, dy, dx: [table[dy, dx, dc] for dc in range(2)]

    def cot_group(g, base, before):
        dy, dx = spots[g]
        return experts_grad(
            g, len(spots), base, both(cots, dy, dx), pair(ranks_t, dy, dx), w_down, cap, mine, before
        )

    def sum_group(stats):
        stats = stats.reshape(2, ng, token_count)
        stats = jnp.concatenate([lax.dynamic_slice_in_dim(stats, inverse[j], 1, 1) for j in range(ng)], 1)
        stats = lax.psum(stats, GROUP)
        stats = jnp.concatenate([lax.dynamic_slice_in_dim(stats, owner[p], 1, 1) for p in range(ng)], 1)
        return stats.reshape(2, ng * token_count)

    starts = [n[0] for n in near]
    raw = dot(normed, w3)
    squares = jnp.stack(
        [jnp.sum(raw[:, i * cols : (i + 1) * cols] ** 2, -1) for i in range(2)]
    )
    cots = [{(0, dx, 0): v for dx, v in n.items()} for n in near]
    for i in range(2):
        cots[i][1, 0, 0] = shift(starts[i], "y", 1)
    squares = sum_group(squares)
    factor = lax.rsqrt(squares / width + EPS).T

    half = HEAD_DIM // 2
    frequencies = jnp.exp(jnp.arange(half, dtype=F32) * (-2.0 * math.log(10000.0) / HEAD_DIM))
    spot = owner[:, None] * span + jnp.arange(span, dtype=jnp.int32)[None, :]
    angles = spot.astype(F32)[:, :, None] * frequencies
    cosine, sine = jnp.cos(angles), jnp.sin(angles)
    cosine = jnp.concatenate([cosine, cosine], -1)
    sine = jnp.concatenate([-sine, sine], -1)
    attention = partial(
        attention_call,
        lengths,
        raw.reshape(ng, seqs, span, -1),
        factor.reshape(ng, seqs, span, 2),
        query_g[None],
        key_g[None],
        cosine,
        sine,
    )
    for dx in range(1, nx):
        cots[0][1, dx, 0] = shift(near[0][dx], "y", 1)
        cots[1][1, dx, 0] = shift(cots[1][1, 0, 0], "x", dx)
    in_turn = [inverse, inverse]
    cots = [with_core(p) for p in cots]
    mixed = [attention(i, 1, inverse=in_turn[i])[0].reshape(ng, span, cols) for i in range(seqs)]
    mixed = [lax.all_to_all(a, GROUP, split_axis=0, concat_axis=0, tiled=True) for a in mixed]
    cot_terms = cot_group(0, base, None)
    parts = []
    for i in range(seqs):
        a = mixed[i].transpose(1, 0, 2).reshape(span, width)
        u = tokens[i].astype(F32) + dot(a, out_full)
        q = lax.rsqrt(jnp.mean(u * u, axis=-1, keepdims=True) + EPS)
        f = (u * q * ffn_g).astype(BF)
        logits = dot(f, router_full)
        weights = jnp.exp(logits - jnp.max(logits, axis=-1, keepdims=True))
        parts.append((a, u, q, f, weights / jnp.sum(weights, axis=-1, keepdims=True)))
    attended, resid, ffn_scale, ffn_in, router = (jnp.concatenate(p, axis=0) for p in zip(*parts))
    ffn_n = resid * ffn_scale

    feats = [{(0, 0, 0): p[3]} for p in parts]
    for i in range(2):
        for dx in range(1, nx):
            feats[i][0, dx, 0] = shift(feats[i][0, 0, 0], "x", dx)
        feats[i][1, 0, 0] = shift(feats[i][0, 0, 0], "y", 1)
        if i == 0:
            row = [feats[0][k] for k in feats[0]]
            row, feats[1][0, 0, 0] = tie(row, feats[1][0, 0, 0])
            feats[0] = dict(zip(feats[0], row))
    base_at, feats[1][0, 0, 0] = tie(base, feats[1][0, 0, 0])
    for g in range(1, len(spots)):
        if g == len(spots) - 1:
            row = [feats[1][k] for k in feats[1]]
            base_at, row, cot_terms = tie(base_at, row, cot_terms)
            feats[1] = dict(zip(feats[1], row))
        cot_terms = cot_group(g, base_at, cot_terms)
    for dx in range(1, nx):
        feats[0][1, dx, 0] = shift(feats[0][0, dx, 0], "y", 1)
        feats[1][1, dx, 0] = shift(feats[1][1, 0, 0], "x", dx)
    gates_t = gather_pair(router.T)

    before, gate_terms = None, {}
    base_at, cot_terms = tie(base, cot_terms)
    feats = [with_core(p) for p in feats]
    og, dhu = cot_terms
    for g, (dy, dx) in enumerate(spots):
        if g == 1:
            row = [[p[k] for k in p] for p in feats]
            base_at, row, before = tie(base_at, row, before)
            feats = [dict(zip(p, v)) for p, v in zip(feats, row)]
        *before, gg = experts_in(
            g, len(spots), base_at, both(feats, dy, dx), pair(ranks_t, dy, dx), pair(gates_t, dy, dx), dhu, w_gate, w_up,
            cap, mine, before,
        )
        gate_terms[dy, dx] = gg
    buf, hg, dg, du = before

    def weight_grad(left, right):
        return lax.dot_general(
            left, right, (((1,), (1,)), ((0,), (0,))), preferred_element_type=F32
        ).astype(BF)

    def finish_part(part):
        rows = part.shape[1] // 2
        keep = lax.dynamic_slice_in_dim(part, y * rows, rows, 1)
        give = shift(lax.dynamic_slice_in_dim(part, (1 - y) * rows, rows, 1), "y", 1)
        return keep, give

    def finish_grad(keep, give):
        first = jnp.where(y == 0, keep, give)
        second = jnp.where(y == 0, give, keep)
        return jnp.concatenate([first, second], axis=0).astype(F32)

    def over_r(value, dim):
        return lax.psum_scatter(value, "r", scatter_dimension=dim, tiled=True)

    first_full, at = tie(weight_grad(og, hg), base)
    scattered = [over_r(first_full, 1)]

    order = list(reversed(list(enumerate(spots))))
    both_ranks = lambda spot: [ranks[*spot, dc] for dc in range(2)]
    top = lambda v: v[:h]
    low = lambda v: v[h:]

    def core_sum(pair):
        return add_low(pair[0], shift(pair[1], "c", 1))

    def first_hops(acc):
        over_x = [shift(top(acc[1, dx]), "x", -dx) for dx in range(1, nx)]
        over_y = [shift(low(acc[1, dx]), "y", 1) for dx in range(1, nx)]
        return over_x, over_y

    def direct(acc):
        return [shift(top(acc[0, dx]), "x", -dx) for dx in range(1, nx)], shift(low(acc[1, 0]), "y", 1)

    def last_hops(acc, hops):
        far = shift(add_low(top(acc[1, 0]), *hops[0]), "y", 1)
        near = [shift(add_low(low(acc[0, dx]), hops[1][dx - 1]), "x", -dx) for dx in range(1, nx)]
        return far, near

    def arrived(acc, straight, last):
        total = lambda terms: sum(t.astype(F32) for t in terms)
        halves = total([top(acc[0, 0]), last[0], *straight[0]]), total([low(acc[0, 0]), straight[1], *last[1]])
        return jnp.concatenate(halves, axis=0)

    back = {}
    for i, (g, spot) in enumerate(order):
        if i >= 2:
            before_last = order[i - 2][1]
            at, back[before_last] = tie(at, back[before_last])
        terms = experts_out(g, at, [dg, du], both_ranks(spot), [w_gate, w_up], cap, mine, False)
        at, terms = tie(at, terms)
        back[spot] = core_sum(terms)
    dg, at = tie(dg, at)
    hops = first_hops(back)
    full = weight_grad(buf, dg)
    full, du, hops = tie(full, du, hops)
    straight = direct(back)
    at, straight, full, scattered[0] = tie(base, straight, full, scattered[0])
    scattered.append(over_r(full, 1))
    mix = {}

    def mix_group(i, at):
        g, spot = order[i]
        mix[spot] = experts_out(g, at, [hg], both_ranks(spot), [w_down], cap, mine, True)
        at, mix[spot] = tie(at, mix[spot])
        return at

    last = last_hops(back, hops)
    for i in range(len(order)):
        if i == len(order) // 2:
            at, last = tie(at, last)
        at = mix_group(i, at)
    dffn = arrived(back, straight, last)

    def swap_y(part):
        keep = lax.dynamic_index_in_dim(part, y, 1, keepdims=False)
        give = lax.dynamic_index_in_dim(part, 1 - y, 1, keepdims=False)
        return keep, shift(give, "y", 1)

    terms = jnp.stack([gate_terms[k] for k in spots])
    terms = terms.reshape(2, nx, mine, 2, token_count)
    pieces = []
    for k in range(2 * ng):
        ty, tx, tc = k // ng, (k % ng) // 2, k % 2
        piece = lax.dynamic_slice(
            terms, ((y - ty) % 2, (x - tx) % nx, 0, (c - tc) % 2, 0), (1, 1, mine, 1, token_count)
        )
        pieces.append(piece.reshape(mine, token_count))
    terms = lax.all_to_all(jnp.stack(pieces), ("y", "x", "c"), split_axis=0, concat_axis=0, tiled=True)
    drouter = terms.reshape(2, ng, mine, token_count).transpose(1, 0, 2, 3).reshape(EXPERTS, token_count).T

    dlogits = router * (drouter - jnp.sum(router * drouter, axis=-1, keepdims=True))
    highest = lax.Precision.HIGHEST
    grad_router = lax.dot_general(ffn_in.astype(F32), dlogits, (((0,), (0,)), ((), ())), precision=highest)
    dffn = dffn + lax.dot_general(
        dlogits, router_full.astype(F32), (((1,), (1,)), ((), ())), precision=highest
    )
    grad_ffn_g = jnp.sum(dffn * ffn_n, axis=0)
    gd = dffn * ffn_g
    dresid = own_cot.astype(F32) + ffn_scale * (gd - ffn_n * jnp.mean(gd * ffn_n, axis=-1, keepdims=True))

    dattn, mix = tie(dresid.astype(BF), mix)
    mix = {k: core_sum(v) for k, v in mix.items()}
    dattended = dot(dattn, out_full, NT).astype(BF)
    dattended = dattended.reshape(token_count, ng, cols).transpose(1, 0, 2).reshape(ng, seqs, span, cols)
    du, dattended = tie(du, dattended)
    dattended = lax.all_to_all(dattended, GROUP, split_axis=0, concat_axis=0, tiled=True)
    full = weight_grad(buf, du)
    grad_out = dot(attended, dattn, TN).astype(BF)
    wrows = w_out.shape[0]
    go = grad_out.reshape(nr * 2, nx, 2, wrows, width)
    keep = lax.dynamic_index_in_dim(go, c, 2, keepdims=False)
    give = lax.dynamic_index_in_dim(go, 1 - c, 2, keepdims=False)
    go = add_low(keep, shift(give, "c", 1))
    parted = [finish_part(scattered[0])]
    hops, straight = first_hops(mix), direct(mix)
    dattended, go, full, scattered[1], hops, straight = tie(dattended, go, full, scattered[1], hops, straight)
    last = last_hops(mix, hops)
    scattered.append(over_r(full, 1))
    dquery, dkey, dvalue, means, gain_grads = attention(0, seqs, inverse, dattended)

    go = add_low(
        *[
            shift(lax.dynamic_index_in_dim(go, (x + dx) % nx, 1, keepdims=False), "x", dx)
            if dx
            else lax.dynamic_index_in_dim(go, x, 1, keepdims=False)
            for dx in range(nx)
        ]
    )
    parted.append(finish_part(scattered[1]))
    dvalue, means, go, parted, last = tie(dvalue.reshape(-1, cols), means, go, parted, last)
    output = (resid + arrived(mix, straight, last)).astype(BF).reshape(seqs, span, width)
    g_value, means = tie(dot(normed, dvalue, TN).astype(BF), means)
    thirds = [swap_y(g_value.reshape(nr, 2, -1, cols))]
    means = sum_group(means.reshape(-1, 2).T).T / width
    gain_grads = gain_grads.sum(axis=0)
    grad_query_g, grad_key_g = gain_grads[0], gain_grads[1]

    def raw_grad(grad, i, gain):
        n = raw[:, i * cols : (i + 1) * cols] * factor[:, i : i + 1]
        return (factor[:, i : i + 1] * (grad.reshape(-1, cols) * gain - n * means[:, i : i + 1])).astype(BF)

    draws = [raw_grad(dquery, 0, query_g), raw_grad(dkey, 1, key_g), dvalue]
    g_pair = dot(normed, jnp.concatenate(draws[:2], axis=1), TN).astype(BF)
    g_pair, thirds[0], go = tie(g_pair, thirds[0], go)
    thirds.append(swap_y(g_pair.reshape(nr, 2, -1, 2 * cols)))
    draw = jnp.concatenate(draws, axis=1)
    dnormed = dot(draw, w3, NT)
    grad_attn_g = jnp.sum(dnormed * normed_n, axis=0)
    thirds[0] = add_low(*thirds[0])
    dnormed, thirds[1], go = tie(dnormed.astype(BF), thirds[1], go)
    go = add_low(*swap_y(go.reshape(nr, 2, wrows, width)))
    thirds[1], grad_attn_g = tie(add_low(*thirds[1]), grad_attn_g)
    dnormed = dnormed.reshape(nx, 2, token_count, width)
    dnormed = [add_low(dnormed[dx, 0], shift(dnormed[dx, 1], "c", 1)) for dx in range(nx)]
    dnormed = sum(
        (shift(dnormed[dx], "x", -dx) if dx else dnormed[0]).astype(F32) for dx in range(nx)
    )
    own_scale = lax.rsqrt(jnp.mean(own_tokens * own_tokens, axis=-1, keepdims=True) + EPS)
    own_n = own_tokens * own_scale
    gd = dnormed * attn_g
    grad_input = dresid + own_scale * (gd - own_n * jnp.mean(gd * own_n, axis=-1, keepdims=True))
    grad_input = grad_input.reshape(seqs, span, width)

    spread = lambda v: lax.dynamic_update_slice(jnp.zeros((width,), F32), v, (me * cols,))
    sums = jnp.concatenate(
        [
            grad_router,
            grad_attn_g[:, None],
            spread(grad_query_g)[:, None],
            spread(grad_key_g)[:, None],
            grad_ffn_g[:, None],
        ],
        axis=1,
    )
    for axis in ALL:
        sums = scatter_small(sums, axis)
    thirds[0], scattered[2] = tie(thirds[0], scattered[2])
    parted.append(finish_part(scattered[2]))
    g_value = over_r(thirds[0], 0)
    g_value, thirds[1] = tie(g_value, thirds[1])
    g_pair = over_r(thirds[1], 0)
    g_pair, go = tie(g_pair, go)
    go = over_r(go, 0)
    g_pair = g_pair.reshape(ng, wrows, 2, cols)
    g_value = g_value.reshape(ng, wrows, 1, cols)
    go = go.reshape(wrows, width).astype(F32)
    g3 = jnp.concatenate([g_pair, g_value], axis=2).transpose(2, 0, 1, 3)
    g3 = lax.all_to_all(g3, GROUP, split_axis=1, concat_axis=1, tiled=True)
    g3 = g3.transpose(0, 2, 1, 3).reshape(3, wrows, width).astype(F32)
    grad_down, grad_gate, grad_up = (finish_grad(*p) for p in parted)
    grad_down = grad_down.transpose(0, 2, 1)

    return (
        output,
        grad_input,
        g3[0],
        g3[1],
        g3[2],
        go,
        sums[:, :EXPERTS],
        sums[:, EXPERTS],
        sums[:, EXPERTS + 1],
        sums[:, EXPERTS + 2],
        sums[:, EXPERTS + 3],
        grad_gate,
        grad_up,
        grad_down,
    )


def solution(mesh):
    ndp, nex = mesh.shape["dp"], mesh.shape["expert"]
    nx = nex // 2
    fine = Mesh(mesh.devices.reshape(ndp // 2, 2, nx, 2), ("r", "y", "x", "c"))
    dp, ex = ("r", "y"), ("x", "c")
    both = dp + ex
    placed = (
        P(dp, ex, None),
        P(dp),
        P(dp, ex, None, None),
        P(both, None),
        P(both, None),
        P(both, None),
        P(both, None),
        P(both, None),
        P(both),
        P(both),
        P(both),
        P(both),
        P(ex, None, None),
        P(ex, None, None),
        P(ex, None, None),
        P(dp, ex, None),
    )
    return jax.shard_map(
        partial(local, nx),
        mesh=fine,
        in_specs=placed,
        out_specs=(
            P(dp, ex, None),
            P(dp, ex, None),
            P(both, None),
            P(both, None),
            P(both, None),
            P(both, None),
            P(both, None),
            P(both),
            P(both),
            P(both),
            P(both),
            P(ex, dp, None),
            P(ex, dp, None),
            P(ex, None, dp),
        ),
        check_vma=False,
    )
```

```python
from functools import partial
import math

import jax
import jax.numpy as jnp
from jax import lax
from jax.experimental import pallas as pl
from jax.experimental.pallas import tpu as pltpu
from jax.sharding import Mesh, PartitionSpec as P

HEAD_DIM = 128
EXPERTS = 16
EPS = 1e-05
F32 = jnp.float32
BF = jnp.bfloat16
VMEM_LIMIT = 60 * 1024 * 1024


def dot(a, b, dims=((1,), (0,))):
    return lax.dot_general(a, b, (dims, ((), ())), preferred_element_type=F32)


NT = ((1,), (1,))
TN = ((0,), (0,))


def masked_scores(q, k, i, j, rows, length, scale):
    s = dot(q, k, NT) * scale
    col = j * rows + lax.broadcasted_iota(jnp.int32, s.shape, 1)
    ok = col < length
    if i == j:
        row = i * rows + lax.broadcasted_iota(jnp.int32, s.shape, 0)
        ok = ok & (col <= row)
    return jnp.where(ok, s, -1e30)


def probs_of(q, key, i, rows, length, scale):
    parts = [masked_scores(q, key[j], i, j, rows, length, scale) for j in range(i + 1)]
    peak = parts[0].max(axis=1, keepdims=True)
    for s in parts[1:]:
        peak = jnp.maximum(peak, s.max(axis=1, keepdims=True))
    parts = [jnp.exp(s - peak) for s in parts]
    total = parts[0].sum(axis=1, keepdims=True)
    for e in parts[1:]:
        total = total + e.sum(axis=1, keepdims=True)
    inverse = 1.0 / total
    return [e * inverse for e in parts]


def turned(v, cosine, sine):
    return v * cosine + pltpu.roll(v, HEAD_DIM // 2, 1) * sine


def normed_turned(raw, factor, gain, cosine, sine):
    return turned(raw * factor * gain, cosine, sine).astype(BF)


def attend_kernel(inv, lens, q_ref, k_ref, v_ref, fac_ref, qg_ref, kg_ref, cos_ref, sin_ref, o_ref, key, *, first, blocks, rows, scale):
    length = lens[first + pl.program_id(0)]
    for i in range(blocks):
        at = inv[i]
        fac, cosine, sine = fac_ref[at], cos_ref[at], sin_ref[at]
        q = normed_turned(q_ref[at], fac[:, 0:1], qg_ref[...], cosine, sine)
        key[i] = normed_turned(k_ref[at], fac[:, 1:2], kg_ref[...], cosine, sine)
        probs = probs_of(q, key, i, rows, length, scale)
        out = jnp.zeros((rows, HEAD_DIM), F32)
        for j, p in enumerate(probs):
            out = out + dot(p.astype(BF), v_ref[inv[j]].astype(BF))
        o_ref[i] = out.astype(BF)


def attend_back_kernel(
    inv, lens, q_ref, k_ref, v_ref, fac_ref, qg_ref, kg_ref, cos_ref, sin_ref, do_ref,
    dq_ref, dk_ref, dv_ref, stat_ref, gain_ref, key, dk_acc, dv_acc, *, first, blocks, rows, scale
):
    length = lens[first + pl.program_id(0)]
    head = pl.program_id(1)
    dk_acc[...] = jnp.zeros_like(dk_acc)
    dv_acc[...] = jnp.zeros_like(dv_acc)

    @pl.when(head == 0)
    def _():
        stat_ref[...] = jnp.zeros_like(stat_ref)

    def unturn(at, grad, raw_ref, which, gain, out_ref):
        grad = turned(grad * scale, cos_ref[at], -sin_ref[at])
        out_ref[at] = grad
        weighted = grad * (raw_ref[at] * fac_ref[at][:, which : which + 1])
        stat_ref[at, :, which : which + 1] += jnp.sum(weighted * gain, axis=1, keepdims=True)
        return jnp.sum(weighted, axis=0, keepdims=True)

    qg, kg = qg_ref[...], kg_ref[...]
    dqg = jnp.zeros((1, HEAD_DIM), F32)
    dkg = jnp.zeros((1, HEAD_DIM), F32)
    for i in range(blocks):
        at = inv[i]
        fac, cosine, sine = fac_ref[at], cos_ref[at], sin_ref[at]
        q = normed_turned(q_ref[at], fac[:, 0:1], qg, cosine, sine)
        key[i] = normed_turned(k_ref[at], fac[:, 1:2], kg, cosine, sine)
        do = do_ref[i]
        probs = probs_of(q, key, i, rows, length, scale)
        dprobs = [dot(do, v_ref[inv[j]].astype(BF), NT) for j in range(i + 1)]
        delta = jnp.zeros((rows, 1), F32)
        for p, dp in zip(probs, dprobs):
            delta = delta + jnp.sum(p * dp, axis=1, keepdims=True)
        dq = jnp.zeros((rows, HEAD_DIM), F32)
        for j, (p, dp) in enumerate(zip(probs, dprobs)):
            ds = (p * (dp - delta)).astype(BF)
            dq = dq + dot(ds, key[j])
            dk_acc[j] += dot(ds, q, TN)
            dv_acc[j] += dot(p.astype(BF), do, TN)
        dqg = dqg + unturn(at, dq, q_ref, 0, qg, dq_ref)
    for j in range(blocks):
        at = inv[j]
        dkg = dkg + unturn(at, dk_acc[j], k_ref, 1, kg, dk_ref)
        dv_ref[at] = dv_acc[j].astype(BF)
    gain_ref[0:1, :] = dqg
    gain_ref[1:2, :] = dkg


def attention_call(lens, raw, factor, query_g, key_g, cosine, sine, first, seqs, inverse, grad=None):
    blocks, _, rows, width = raw.shape
    heads = width // (3 * HEAD_DIM)
    part = lambda k: pl.BlockSpec((blocks, None, rows, HEAD_DIM), lambda s, h, *_: (0, first + s, 0, k * heads + h))
    out = pl.BlockSpec((blocks, None, rows, HEAD_DIM), lambda s, h, *_: (0, s, 0, h))
    fac = pl.BlockSpec((blocks, None, rows, 2), lambda s, h, *_: (0, first + s, 0, 0))
    gain = pl.BlockSpec((1, HEAD_DIM), lambda s, h, *_: (0, h))
    turn = pl.BlockSpec((blocks, rows, HEAD_DIM), lambda s, h, *_: (0, 0, 0))
    ins = [raw, raw, raw, factor, query_g, key_g, cosine, sine]
    in_specs = [part(0), part(1), part(2), fac, gain, gain, turn, turn]
    one = (blocks, seqs, rows, width // 3)
    shape = jax.ShapeDtypeStruct
    scratch = [pltpu.VMEM((blocks, rows, HEAD_DIM), BF)]
    flops = 2 * 2 * (blocks * rows) ** 2 * seqs * width // 3 * 5 // 8
    if grad is None:
        kernel, outs, out_specs = attend_kernel, [shape(one, BF)], [out]
    else:
        ins, in_specs = ins + [grad], in_specs + [out]
        kernel = attend_back_kernel
        outs = [shape(one, F32), shape(one, F32), shape(one, BF)]
        outs += [shape((blocks, seqs, rows, 2), F32), shape((seqs, 2, width // 3), F32)]
        out_specs = [out] * 3 + [fac, pl.BlockSpec((None, 2, HEAD_DIM), lambda s, h, *_: (s, 0, h))]
        scratch += [pltpu.VMEM((blocks, rows, HEAD_DIM), F32)] * 2
        flops = flops * 5 // 2
    return pl.pallas_call(
        partial(kernel, first=first, blocks=blocks, rows=rows, scale=1.0 / math.sqrt(HEAD_DIM)),
        out_shape=outs,
        grid_spec=pltpu.PrefetchScalarGridSpec(
            num_scalar_prefetch=2, grid=(seqs, heads), in_specs=in_specs, out_specs=out_specs, scratch_shapes=scratch
        ),
        compiler_params=pltpu.CompilerParams(vmem_limit_bytes=VMEM_LIMIT),
        cost_estimate=pl.CostEstimate(
            flops=flops, bytes_accessed=raw.size * 6, transcendentals=(blocks * rows) ** 2 * seqs * heads * 5 // 8
        ),
    )(inverse, lens, *ins)


def pick_row(table, index):
    which = lax.broadcasted_iota(jnp.int32, table.shape, 0) == index
    return jnp.sum(jnp.where(which, table, 0.0), axis=0, keepdims=True)


def selection(rank_table, expert, cap):
    rank = pick_row(rank_table, expert)
    return lax.broadcasted_iota(jnp.int32, (cap, rank.shape[1]), 0).astype(F32) == rank


def dispatch(out, b, s, top, low, cap):
    half = top.shape[0]
    s = s.astype(F32).astype(BF)
    out[pl.ds(b * cap, cap), :] = (dot(s[:, :half], top[...]) + dot(s[:, half:], low[...])).astype(BF)


def experts_grad_kernel(base, *refs, cap, groups):
    pieces, wd, (og, dh) = refs[: 6 * groups], refs[6 * groups], refs[-2:]
    expert = base[1] + pl.program_id(0)
    for k in range(groups):

        @pl.when(pl.program_id(1) == k)
        def _():
            c00, c01, c10, c11, r0, r1 = pieces[6 * k : 6 * k + 6]
            for b, (r, top, low) in enumerate(((r0, c00, c01), (r1, c10, c11))):
                dispatch(og, b, selection(r[...], expert, cap), top, low, cap)

    ff = wd.shape[0]
    for at in range(0, ff, 512):
        cols = slice(at, min(at + 512, ff))
        dh[:, cols] = dot(og[...], wd[cols, :], NT)


def experts_in_kernel(base, *refs, cap, groups):
    pieces, (dhu, wg, wu) = refs[: 8 * groups], refs[8 * groups : 8 * groups + 3]
    buf, hg, dg, du, gg, weight, dots = refs[-7:]
    expert = base[1] + pl.program_id(0)
    for k in range(groups):

        @pl.when(pl.program_id(1) == k)
        def _():
            f00, f01, f10, f11, r0, r1, g0, g1 = pieces[8 * k : 8 * k + 8]
            for b, (r, g, top, low) in enumerate(((r0, g0, f00, f01), (r1, g1, f10, f11))):
                s = selection(r[...], expert, cap)
                dispatch(buf, b, s, top, low, cap)
                gate = pick_row(g[...], expert)
                weight[pl.ds(b * cap, cap), :] = jnp.sum(jnp.where(s, gate, 0.0), axis=1, keepdims=True)

    ff = wg.shape[1]
    total = None
    for at in range(0, ff, 512):
        cols = slice(at, min(at + 512, ff))
        x = buf[...]
        gate = dot(x, wg[:, cols])
        up = dot(x, wu[:, cols])
        dh = dhu[:, cols]
        w = weight[...]
        sg = 1.0 / (1.0 + jnp.exp(-gate))
        silu = gate * sg
        hidden = (silu * up).astype(BF).astype(F32)
        part = jnp.sum(hidden * dh, axis=1, keepdims=True)
        total = part if total is None else total + part
        dh = dh * w
        hg[:, cols] = (hidden * w).astype(BF)
        dg[:, cols] = (dh * up * (sg * (1.0 + gate * (1.0 - sg)))).astype(BF)
        du[:, cols] = (dh * silu).astype(BF)
    dots[...] = total
    for k in range(groups):

        @pl.when(pl.program_id(1) == k)
        def _():
            for b, r in enumerate(pieces[8 * k + 4 : 8 * k + 6]):
                s = selection(r[...], expert, cap)
                gg[b] = jnp.sum(jnp.where(s, dots[pl.ds(b * cap, cap), :], 0.0), axis=0, keepdims=True)


def experts_call(kernel, first, total, base, small, wide_ins, weights, wide_outs, gates, cap, local, before, flops):
    groups = len(small)
    width = weights[-1].shape[1] if gates else weights[-1].shape[2]
    ff = weights[-1].shape[2] if gates else weights[-1].shape[1]
    rows = 2 * cap
    tokens = small[0][0].shape[0] * 2
    small = [a for group in small for a in group]
    whole = lambda a: pl.BlockSpec(a.shape, lambda e, g, s: (0, 0), pipeline_mode=pl.Buffered(1))
    wide = pl.BlockSpec((None, rows, width), lambda e, g, s: (e, first + g, 0))
    thin = pl.BlockSpec((None, rows, ff), lambda e, g, s: (e, first + g, 0))
    heavy = pl.BlockSpec((None, *weights[-1].shape[1:]), lambda e, g, s: (s[0] + e, 0, 0))
    shape = jax.ShapeDtypeStruct
    outs = [shape((local, total * rows, width if w else ff), t) for w, t in wide_outs]
    out_specs = [wide if w else thin for w, _ in wide_outs]
    scratch = []
    if gates:
        outs.append(shape((local, groups, 2, 1, tokens), F32))
        out_specs.append(pl.BlockSpec((None, None, 2, 1, tokens), lambda e, g, s: (e, g, 0, 0, 0)))
        scratch = [pltpu.VMEM((rows, 1), F32)] * 2
    before = [] if before is None else before
    n = 1 + len(small) + len(wide_ins) + len(weights)
    return pl.pallas_call(
        partial(kernel, cap=cap, groups=groups),
        out_shape=outs,
        grid_spec=pltpu.PrefetchScalarGridSpec(
            num_scalar_prefetch=1,
            grid=(local, groups),
            in_specs=[whole(a) for a in small]
            + [thin] * len(wide_ins)
            + [heavy] * len(weights)
            + [pl.BlockSpec(memory_space=pl.ANY)] * len(before),
            out_specs=out_specs,
            scratch_shapes=scratch,
        ),
        input_output_aliases={n + i: i for i in range(len(before))},
        compiler_params=pltpu.CompilerParams(vmem_limit_bytes=VMEM_LIMIT),
        cost_estimate=pl.CostEstimate(
            flops=groups * flops,
            bytes_accessed=local * (len(weights) * width * ff * 2 + groups * rows * (2 * width + 10 * ff))
            + groups * 4 * tokens * width,
            transcendentals=groups * local * rows * ff if gates else 0,
        ),
    )(base, *small, *wide_ins, *weights, *before)


def experts_grad(first, total, base, small, wd, cap, local, before):
    flops = local * 2 * cap * wd.shape[2] * (2 * wd.shape[1] + 4 * small[0][0].shape[0])
    return experts_call(
        experts_grad_kernel, first, total, base, small, [], [wd], [(True, BF), (False, F32)],
        False, cap, local, before, flops,
    )


def experts_in(first, total, base, small, dhu, wg, wu, cap, local, before):
    flops = local * 2 * cap * wg.shape[1] * (4 * wg.shape[2] + 4 * small[0][0].shape[0])
    return experts_call(
        experts_in_kernel, first, total, base, small, [dhu], [wg, wu],
        [(True, BF), (False, BF), (False, BF), (False, BF)], True, cap, local, before, flops,
    )


def experts_out_kernel(base, *refs, cap, forward):
    if forward:
        hg, r0, r1, wd, t0, t1 = refs
        parts = [dot(hg[e], wd[e]).astype(BF) for e in range(hg.shape[0])]
    else:
        dg, du, r0, r1, wg, wu, t0, t1 = refs
        parts = [(dot(dg[e], wg[e], NT) + dot(du[e], wu[e], NT)).astype(BF) for e in range(dg.shape[0])]
    for b, (rank, final) in enumerate(((r0, t0), (r1, t1))):
        table = rank[...]
        total = None
        for e, part in enumerate(parts):
            which = lax.broadcasted_iota(jnp.int32, table.shape, 1) == base[1] + e
            column = jnp.sum(jnp.where(which, table, 0.0), axis=1, keepdims=True)
            slot = lax.broadcasted_iota(jnp.int32, (table.shape[0], cap), 1).astype(F32)
            pick = (slot == column).astype(F32).astype(BF)
            term = dot(pick, part[b * cap : (b + 1) * cap])
            total = term if total is None else total + term
        final[...] = total.astype(BF)


def experts_out(group, base, rows_in, ranks, weights, cap, local, forward):
    tokens = ranks[0].shape[0]
    width, ff = weights[0].shape[1:]
    if forward:
        ff, width = width, ff
    tile = 512
    rows = 2 * cap
    thin = pl.BlockSpec((local, rows, ff), lambda d, s: (0, group, 0))
    whole = pl.BlockSpec((tokens, EXPERTS), lambda d, s: (0, 0))
    final = pl.BlockSpec((tokens, tile), lambda d, s: (0, d))
    if forward:
        heavy = pl.BlockSpec((local, ff, tile), lambda d, s: (s[2], 0, d))
    else:
        heavy = pl.BlockSpec((local, tile, ff), lambda d, s: (s[2], d, 0))
    n = len(weights)
    return pl.pallas_call(
        partial(experts_out_kernel, cap=cap, forward=forward),
        out_shape=[jax.ShapeDtypeStruct((tokens, width), BF)] * 2,
        grid_spec=pltpu.PrefetchScalarGridSpec(
            num_scalar_prefetch=1,
            grid=(width // tile,),
            in_specs=[thin] * n + [whole] * 2 + [heavy] * n,
            out_specs=[final] * 2,
        ),
        compiler_params=pltpu.CompilerParams(vmem_limit_bytes=VMEM_LIMIT),
        cost_estimate=pl.CostEstimate(
            flops=local * rows * width * (2 * n * ff + 2 * tokens),
            bytes_accessed=local * n * (width * ff + rows * ff) * 2 + 4 * tokens * width,
            transcendentals=0,
        ),
    )(base, *rows_in, *ranks, *weights)


def shift(value, axis, by):
    n = lax.axis_size(axis)
    return lax.ppermute(value, axis, [(i, (i + by) % n) for i in range(n)])


def gather_small(value, axis):
    n, index, rows = lax.axis_size(axis), lax.axis_index(axis), value.shape[0]
    out = jnp.zeros((n * rows, *value.shape[1:]), value.dtype)
    for by in range(n):
        piece = shift(value, axis, by) if by else value
        out = lax.dynamic_update_slice_in_dim(out, piece, (index - by) % n * rows, 0)
    return out


def scatter_small(value, axis):
    n, index = lax.axis_size(axis), lax.axis_index(axis)
    value = value.reshape(n, -1, *value.shape[1:])
    part = lambda i: lax.dynamic_index_in_dim(value, i % n, 0, keepdims=False)
    total = part(index)
    for by in range(1, n):
        total = total + shift(part(index + by), axis, by)
    return total


def tie(*values):
    return lax.optimization_barrier(values)


def add_low(*terms):
    total = terms[0].astype(F32)
    for t in terms[1:]:
        total = total + t.astype(F32)
    return total.astype(BF)


def rms_parts(values):
    return values * lax.rsqrt(jnp.mean(values * values, axis=-1, keepdims=True) + EPS)


def local(
    nx,
    tokens,
    lengths,
    routes,
    w_query,
    w_key,
    w_value,
    w_out,
    w_router,
    attn_gain,
    query_gain,
    key_gain,
    ffn_gain,
    w_gate,
    w_up,
    w_down,
    cotangent,
):
    ALL, GROUP = ("r", "y", "x", "c"), ("x", "c")
    r, y, x, c = (lax.axis_index(a) for a in ALL)
    nr = lax.axis_size("r")
    me = 2 * x + c
    ng = 2 * nx
    seqs, span, width = tokens.shape
    token_count = seqs * span
    top_count = routes.shape[-1]
    cap = (token_count * top_count * 9 + 8 * EXPERTS - 1) // (8 * EXPERTS)
    cols = width // ng
    length = span * ng
    places = [(dx, dc) for dx in range(nx) for dc in range(2)]
    owner = jnp.stack([2 * ((x - dx) % nx) + (c - dc) % 2 for dx, dc in places]).astype(jnp.int32)
    inverse = jnp.stack(
        [2 * ((x - j // 2) % nx) + (c - j % 2) % 2 for j in range(ng)]
    ).astype(jnp.int32)

    w3 = jnp.stack([w_query, w_key, w_value], axis=1).reshape(-1, 3, ng, cols)
    w3 = w3.transpose(2, 0, 1, 3).reshape(ng, -1, 3 * cols)
    w3 = lax.all_to_all(w3, GROUP, split_axis=0, concat_axis=0, tiled=True)
    w3 = lax.all_gather(w3.reshape(-1, 3 * cols), ("r", "y"), axis=0, tiled=True)
    extras = jnp.concatenate(
        [w_router, attn_gain[:, None], query_gain[:, None], key_gain[:, None], ffn_gain[:, None]], axis=1
    )
    for axis in reversed(ALL):
        extras = gather_small(extras, axis)
    out_full = lax.all_gather(w_out, ALL, axis=0, tiled=True)
    router_full = extras[:, :EXPERTS]
    attn_g, query_g, key_g, ffn_g = (extras[:, EXPERTS + i].astype(F32) for i in range(4))
    query_g = lax.dynamic_slice(query_g, (me * cols,), (cols,))
    key_g = lax.dynamic_slice(key_g, (me * cols,), (cols,))

    choose = routes.reshape(token_count, top_count)
    chosen = jnp.sum(
        (choose[:, :, None] == jnp.arange(EXPERTS, dtype=jnp.int32)).astype(F32), axis=1
    )
    tri = (
        lax.broadcasted_iota(jnp.int32, (token_count, token_count), 0)
        > lax.broadcasted_iota(jnp.int32, (token_count, token_count), 1)
    ).astype(BF)
    rank = jnp.where(chosen > 0, dot(tri, chosen.astype(BF)), -1.0)

    def gather_group(value):
        pieces = []
        for dx in range(nx):
            far = shift(value, "x", dx) if dx else value
            pieces += [far, shift(far, "c", 1)]
        return pieces

    own_places = me * span + jnp.arange(span, dtype=jnp.int32)
    valid = (own_places[None, :] < lengths[:, None]).reshape(token_count)
    own_cot = jnp.where(valid[:, None], cotangent.reshape(token_count, width), jnp.zeros((), BF))
    own_tokens = tokens.astype(F32).reshape(token_count, width)

    all_tokens = jnp.stack(gather_group(tokens)).reshape(ng * token_count, width).astype(F32)
    h = token_count // 2
    cot_halves = [own_cot[:h], own_cot[h:]]
    near = [{dx: shift(v, "x", dx) if dx else v for dx in range(nx)} for v in cot_halves]
    normed_n = rms_parts(all_tokens)
    normed = (normed_n * attn_g).astype(BF)

    spots = [(dy, dx) for dy in range(2) for dx in range(nx)]

    def gather_pair(value):
        out = {(0, 0): value}
        for dx in range(1, nx):
            out[0, dx] = shift(value, "x", dx)
        for dx in range(nx):
            out[1, dx] = shift(out[0, dx], "y", 1)
        return {(dy, dx, dc): shift(v, "c", 1) if dc else v for (dy, dx), v in out.items() for dc in range(2)}

    def with_core(pieces):
        return pieces | {(dy, dx, 1): shift(v, "c", 1) for (dy, dx, _), v in pieces.items()}

    ranks_t = gather_pair(rank.T)
    ranks = {k: v.T for k, v in ranks_t.items()}
    w3, normed, ranks_t, near[0] = tie(w3, normed, ranks_t, near[0])

    local_experts = w_gate.shape[0]
    mine = local_experts // 2
    base = jnp.stack([y * mine, me * local_experts + y * mine, y]).astype(jnp.int32)
    both = lambda halves, dy, dx: [halves[h][dy, dx, dc] for dc in range(2) for h in range(2)]
    pair = lambda table, dy, dx: [table[dy, dx, dc] for dc in range(2)]

    close, far = spots[:nx], spots[nx:]

    def cot_call(chips, base, before):
        small = [[*both(cots, *k), *pair(ranks_t, *k)] for k in chips]
        return experts_grad(spots.index(chips[0]), len(spots), base, small, w_down, cap, mine, before)

    def in_call(chips, base, before):
        small = [[*both(feats, *k), *pair(ranks_t, *k), *pair(gates_t, *k)] for k in chips]
        return experts_in(spots.index(chips[0]), len(spots), base, small, dhu, w_gate, w_up, cap, mine, before)

    def sum_group(stats):
        stats = stats.reshape(2, ng, token_count)
        stats = jnp.concatenate([lax.dynamic_slice_in_dim(stats, inverse[j], 1, 1) for j in range(ng)], 1)
        stats = lax.psum(stats, GROUP)
        stats = jnp.concatenate([lax.dynamic_slice_in_dim(stats, owner[p], 1, 1) for p in range(ng)], 1)
        return stats.reshape(2, ng * token_count)

    starts = [n[0] for n in near]
    raw = dot(normed, w3)
    squares = jnp.stack(
        [jnp.sum(raw[:, i * cols : (i + 1) * cols] ** 2, -1) for i in range(2)]
    )
    across = [shift(v, "y", 1) for v in starts]
    squares, near[1] = tie(squares, near[1])
    squares = sum_group(squares)
    factor = lax.rsqrt(squares / width + EPS).T

    half = HEAD_DIM // 2
    frequencies = jnp.exp(jnp.arange(half, dtype=F32) * (-2.0 * math.log(10000.0) / HEAD_DIM))
    spot = owner[:, None] * span + jnp.arange(span, dtype=jnp.int32)[None, :]
    angles = spot.astype(F32)[:, :, None] * frequencies
    cosine, sine = jnp.cos(angles), jnp.sin(angles)
    cosine = jnp.concatenate([cosine, cosine], -1)
    sine = jnp.concatenate([-sine, sine], -1)
    attention = partial(
        attention_call,
        lengths,
        raw.reshape(ng, seqs, span, -1),
        factor.reshape(ng, seqs, span, 2),
        query_g[None],
        key_g[None],
        cosine,
        sine,
    )
    second, across[0] = tie(inverse, across[0])
    in_turn = [inverse, second]
    mixed = [attention(i, 1, inverse=in_turn[i])[0].reshape(ng, span, cols) for i in range(seqs)]
    mixed = [lax.all_to_all(a, GROUP, split_axis=0, concat_axis=0, tiled=True) for a in mixed]
    mixed[0], across[1] = tie(mixed[0], across[1])
    corner = [[shift(near[0][dx], "y", 1) for dx in range(1, nx)], [shift(across[1], "x", dx) for dx in range(1, nx)]]
    mixed[1], corner = tie(mixed[1], corner)
    cots = [{(0, dx, 0): v for dx, v in n.items()} for n in near]
    for i in range(2):
        cots[i][1, 0, 0] = across[i]
        for dx in range(1, nx):
            cots[i][1, dx, 0] = corner[i][dx - 1]
    cots = [with_core(p) for p in cots]
    cot_terms = cot_call(close, base, None)
    parts = []
    for i in range(seqs):
        a = mixed[i].transpose(1, 0, 2).reshape(span, width)
        u = tokens[i].astype(F32) + dot(a, out_full)
        q = lax.rsqrt(jnp.mean(u * u, axis=-1, keepdims=True) + EPS)
        f = (u * q * ffn_g).astype(BF)
        logits = dot(f, router_full)
        weights = jnp.exp(logits - jnp.max(logits, axis=-1, keepdims=True))
        parts.append((a, u, q, f, weights / jnp.sum(weights, axis=-1, keepdims=True)))
    attended, resid, ffn_scale, ffn_in, router = (jnp.concatenate(p, axis=0) for p in zip(*parts))
    ffn_n = resid * ffn_scale

    feats = [{(0, 0, 0): p[3]} for p in parts]
    for i in range(2):
        for dx in range(1, nx):
            feats[i][0, dx, 0] = shift(feats[i][0, 0, 0], "x", dx)
        feats[i][1, 0, 0] = shift(feats[i][0, 0, 0], "y", 1)
        if i == 0:
            row = [feats[0][k] for k in feats[0]]
            row, feats[1][0, 0, 0] = tie(row, feats[1][0, 0, 0])
            feats[0] = dict(zip(feats[0], row))
    base_at, feats[1][0, 0, 0] = tie(base, feats[1][0, 0, 0])
    cot_terms = cot_call(far, base_at, cot_terms)
    for dx in range(1, nx):
        feats[0][1, dx, 0] = shift(feats[0][0, dx, 0], "y", 1)
        feats[1][1, dx, 0] = shift(feats[1][1, 0, 0], "x", dx)
    gates_t = gather_pair(router.T)

    base_at, cot_terms = tie(base, cot_terms)
    og, dhu = cot_terms
    feats = [with_core(p) for p in feats]
    *before, gg = in_call(close, base_at, None)
    gate_terms = dict(zip(close, [gg[:, k] for k in range(nx)]))
    row = [[p[k] for k in p] for p in feats]
    base_at, row, before = tie(base_at, row, before)
    feats = [dict(zip(p, v)) for p, v in zip(feats, row)]
    *before, gg = in_call(far, base_at, before)
    gate_terms |= dict(zip(far, [gg[:, k] for k in range(nx)]))
    buf, hg, dg, du = before

    def weight_grad(left, right):
        return lax.dot_general(
            left, right, (((1,), (1,)), ((0,), (0,))), preferred_element_type=F32
        ).astype(BF)

    def finish_part(part):
        rows = part.shape[1] // 2
        keep = lax.dynamic_slice_in_dim(part, y * rows, rows, 1)
        give = shift(lax.dynamic_slice_in_dim(part, (1 - y) * rows, rows, 1), "y", 1)
        return keep, give

    def finish_grad(keep, give):
        first = jnp.where(y == 0, keep, give)
        second = jnp.where(y == 0, give, keep)
        return jnp.concatenate([first, second], axis=0).astype(F32)

    def over_r(value, dim):
        return lax.psum_scatter(value, "r", scatter_dimension=dim, tiled=True)

    first_full, at = tie(weight_grad(og, hg), base)
    scattered = [over_r(first_full, 1)]

    order = list(reversed(list(enumerate(spots))))
    both_ranks = lambda spot: [ranks[*spot, dc] for dc in range(2)]
    top = lambda v: v[:h]
    low = lambda v: v[h:]

    def core_sum(pair):
        return add_low(pair[0], shift(pair[1], "c", 1))

    def first_hops(acc):
        over_x = [shift(top(acc[1, dx]), "x", -dx) for dx in range(1, nx)]
        over_y = [shift(low(acc[1, dx]), "y", 1) for dx in range(1, nx)]
        return over_x, over_y

    def direct(acc):
        return [shift(top(acc[0, dx]), "x", -dx) for dx in range(1, nx)], shift(low(acc[1, 0]), "y", 1)

    def last_hops(acc, hops):
        far = shift(add_low(top(acc[1, 0]), *hops[0]), "y", 1)
        near = [shift(add_low(low(acc[0, dx]), hops[1][dx - 1]), "x", -dx) for dx in range(1, nx)]
        return far, near

    def arrived(acc, straight, last):
        total = lambda terms: sum(t.astype(F32) for t in terms)
        halves = total([top(acc[0, 0]), last[0], *straight[0]]), total([low(acc[0, 0]), straight[1], *last[1]])
        return jnp.concatenate(halves, axis=0)

    back = {}
    for i, (g, spot) in enumerate(order):
        if i >= 2:
            before_last = order[i - 2][1]
            at, back[before_last] = tie(at, back[before_last])
        terms = experts_out(g, at, [dg, du], both_ranks(spot), [w_gate, w_up], cap, mine, False)
        at, terms = tie(at, terms)
        back[spot] = core_sum(terms)
    dg, at = tie(dg, at)
    hops = first_hops(back)
    full = weight_grad(buf, dg)
    full, du, hops = tie(full, du, hops)
    straight = direct(back)
    at, straight = tie(base, straight)
    mix = {}

    def mix_group(i, at):
        g, spot = order[i]
        mix[spot] = experts_out(g, at, [hg], both_ranks(spot), [w_down], cap, mine, True)
        at, mix[spot] = tie(at, mix[spot])
        return at

    last = last_hops(back, hops)
    for i in range(len(order)):
        if i == 1:
            at, full, scattered[0] = tie(at, full, scattered[0])
            scattered.append(over_r(full, 1))
        if i == len(order) // 2:
            at, last = tie(at, last)
        at = mix_group(i, at)
    dffn = arrived(back, straight, last)

    def parts_y(part):
        return [lax.dynamic_index_in_dim(part, i, 1, keepdims=False) for i in (y, 1 - y)]

    def swap_y(part):
        keep, give = parts_y(part)
        return keep, shift(give, "y", 1)

    terms = jnp.stack([gate_terms[k] for k in spots])
    terms = terms.reshape(2, nx, mine, 2, token_count)
    pieces = []
    for k in range(2 * ng):
        ty, tx, tc = k // ng, (k % ng) // 2, k % 2
        piece = lax.dynamic_slice(
            terms, ((y - ty) % 2, (x - tx) % nx, 0, (c - tc) % 2, 0), (1, 1, mine, 1, token_count)
        )
        pieces.append(piece.reshape(mine, token_count))
    terms = lax.all_to_all(jnp.stack(pieces), ("y", "x", "c"), split_axis=0, concat_axis=0, tiled=True)
    drouter = terms.reshape(2, ng, mine, token_count).transpose(1, 0, 2, 3).reshape(EXPERTS, token_count).T

    dlogits = router * (drouter - jnp.sum(router * drouter, axis=-1, keepdims=True))
    highest = lax.Precision.HIGHEST
    grad_router = lax.dot_general(ffn_in.astype(F32), dlogits, (((0,), (0,)), ((), ())), precision=highest)
    dffn = dffn + lax.dot_general(
        dlogits, router_full.astype(F32), (((1,), (1,)), ((), ())), precision=highest
    )
    grad_ffn_g = jnp.sum(dffn * ffn_n, axis=0)
    gd = dffn * ffn_g
    dresid = own_cot.astype(F32) + ffn_scale * (gd - ffn_n * jnp.mean(gd * ffn_n, axis=-1, keepdims=True))

    dattn, mix = tie(dresid.astype(BF), mix)
    mix = {k: core_sum(v) for k, v in mix.items()}
    dattended = dot(dattn, out_full, NT).astype(BF)
    dattended = dattended.reshape(token_count, ng, cols).transpose(1, 0, 2).reshape(ng, seqs, span, cols)
    du, dattended = tie(du, dattended)
    dattended = lax.all_to_all(dattended, GROUP, split_axis=0, concat_axis=0, tiled=True)
    full = weight_grad(buf, du)
    grad_out = dot(attended, dattn, TN).astype(BF)
    wrows = w_out.shape[0]
    go = grad_out.reshape(nr * 2, nx, 2, wrows, width)
    keep = lax.dynamic_index_in_dim(go, c, 2, keepdims=False)
    give = lax.dynamic_index_in_dim(go, 1 - c, 2, keepdims=False)
    go = add_low(keep, shift(give, "c", 1))
    parted = [finish_part(scattered[0])]
    hops, straight = first_hops(mix), direct(mix)
    dattended, go, full, scattered[1] = tie(dattended, go, full, scattered[1])
    scattered.append(over_r(full, 1))
    dattended, hops, straight = tie(dattended, hops, straight)
    last = last_hops(mix, hops)
    dquery, dkey, dvalue, means, gain_grads = attention(0, seqs, inverse, dattended)

    go = add_low(
        *[
            shift(lax.dynamic_index_in_dim(go, (x + dx) % nx, 1, keepdims=False), "x", dx)
            if dx
            else lax.dynamic_index_in_dim(go, x, 1, keepdims=False)
            for dx in range(nx)
        ]
    )
    parted.append(finish_part(scattered[1]))
    dvalue, means, go, parted, last = tie(dvalue.reshape(-1, cols), means, go, parted, last)
    output = (resid + arrived(mix, straight, last)).astype(BF).reshape(seqs, span, width)
    g_value, means = tie(dot(normed, dvalue, TN).astype(BF), means)
    thirds = [swap_y(g_value.reshape(nr, 2, -1, cols))]
    means = sum_group(means.reshape(-1, 2).T).T / width
    gain_grads = gain_grads.sum(axis=0)
    grad_query_g, grad_key_g = gain_grads[0], gain_grads[1]

    def raw_grad(grad, i, gain):
        n = raw[:, i * cols : (i + 1) * cols] * factor[:, i : i + 1]
        return (factor[:, i : i + 1] * (grad.reshape(-1, cols) * gain - n * means[:, i : i + 1])).astype(BF)

    draws = [raw_grad(dquery, 0, query_g), raw_grad(dkey, 1, key_g), dvalue]
    g_pair = dot(normed, jnp.concatenate(draws[:2], axis=1), TN).astype(BF)
    keep, give = parts_y(g_pair.reshape(nr, 2, -1, 2 * cols))
    keep, give, thirds[0], draws = tie(keep, give, thirds[0], draws)
    thirds.append((keep, shift(give, "y", 1)))
    draw = jnp.concatenate(draws, axis=1)
    dnormed = dot(draw, w3, NT)
    grad_attn_g = jnp.sum(dnormed * normed_n, axis=0)
    g_value, scattered[2] = tie(add_low(*thirds[0]), scattered[2])
    g_value = over_r(g_value, 0)
    spread = lambda v: lax.dynamic_update_slice(jnp.zeros((width,), F32), v, (me * cols,))
    sums = jnp.concatenate(
        [
            grad_router,
            grad_attn_g[:, None],
            spread(grad_query_g)[:, None],
            spread(grad_key_g)[:, None],
            grad_ffn_g[:, None],
        ],
        axis=1,
    )
    for axis in ALL:
        sums = scatter_small(sums, axis)
    dnormed, thirds[1], go, sums, g_value = tie(dnormed.astype(BF), thirds[1], go, sums, g_value)
    go = add_low(*swap_y(go.reshape(nr, 2, wrows, width)))
    thirds[1] = add_low(*thirds[1])
    dnormed = dnormed.reshape(nx, 2, token_count, width)
    dnormed = [add_low(dnormed[dx, 0], shift(dnormed[dx, 1], "c", 1)) for dx in range(nx)]
    dnormed = sum(
        (shift(dnormed[dx], "x", -dx) if dx else dnormed[0]).astype(F32) for dx in range(nx)
    )
    own_scale = lax.rsqrt(jnp.mean(own_tokens * own_tokens, axis=-1, keepdims=True) + EPS)
    own_n = own_tokens * own_scale
    gd = dnormed * attn_g
    grad_input = dresid + own_scale * (gd - own_n * jnp.mean(gd * own_n, axis=-1, keepdims=True))
    grad_input = grad_input.reshape(seqs, span, width)

    g_pair, go, scattered[2] = tie(over_r(thirds[1], 0), go, scattered[2])
    go = over_r(go, 0)
    parted.append(finish_part(scattered[2]))
    g_pair = g_pair.reshape(ng, wrows, 2, cols)
    g_value = g_value.reshape(ng, wrows, 1, cols)
    go = go.reshape(wrows, width).astype(F32)
    g3 = jnp.concatenate([g_pair, g_value], axis=2).transpose(2, 0, 1, 3)
    g3 = lax.all_to_all(g3, GROUP, split_axis=1, concat_axis=1, tiled=True)
    g3 = g3.transpose(0, 2, 1, 3).reshape(3, wrows, width).astype(F32)
    grad_down, grad_gate, grad_up = (finish_grad(*p) for p in parted)
    grad_down = grad_down.transpose(0, 2, 1)

    return (
        output,
        grad_input,
        g3[0],
        g3[1],
        g3[2],
        go,
        sums[:, :EXPERTS],
        sums[:, EXPERTS],
        sums[:, EXPERTS + 1],
        sums[:, EXPERTS + 2],
        sums[:, EXPERTS + 3],
        grad_gate,
        grad_up,
        grad_down,
    )


def solution(mesh):
    ndp, nex = mesh.shape["dp"], mesh.shape["expert"]
    nx = nex // 2
    fine = Mesh(mesh.devices.reshape(ndp // 2, 2, nx, 2), ("r", "y", "x", "c"))
    dp, ex = ("r", "y"), ("x", "c")
    both = dp + ex
    placed = (
        P(dp, ex, None),
        P(dp),
        P(dp, ex, None, None),
        P(both, None),
        P(both, None),
        P(both, None),
        P(both, None),
        P(both, None),
        P(both),
        P(both),
        P(both),
        P(both),
        P(ex, None, None),
        P(ex, None, None),
        P(ex, None, None),
        P(dp, ex, None),
    )
    return jax.shard_map(
        partial(local, nx),
        mesh=fine,
        in_specs=placed,
        out_specs=(
            P(dp, ex, None),
            P(dp, ex, None),
            P(both, None),
            P(both, None),
            P(both, None),
            P(both, None),
            P(both, None),
            P(both),
            P(both),
            P(both),
            P(both),
            P(ex, dp, None),
            P(ex, dp, None),
            P(ex, None, dp),
        ),
        check_vma=False,
    )
```

```python
from functools import partial
import math

import jax
import jax.numpy as jnp
from jax import lax
from jax.experimental import pallas as pl
from jax.experimental.pallas import tpu as pltpu
from jax.sharding import Mesh, PartitionSpec as P

HEAD_DIM = 128
EXPERTS = 16
EPS = 1e-05
F32 = jnp.float32
BF = jnp.bfloat16
VMEM_LIMIT = 60 * 1024 * 1024


def dot(a, b, dims=((1,), (0,))):
    return lax.dot_general(a, b, (dims, ((), ())), preferred_element_type=F32)


NT = ((1,), (1,))
TN = ((0,), (0,))


def masked_scores(q, k, i, j, rows, length, scale):
    s = dot(q, k, NT) * scale
    col = j * rows + lax.broadcasted_iota(jnp.int32, s.shape, 1)
    ok = col < length
    if i == j:
        row = i * rows + lax.broadcasted_iota(jnp.int32, s.shape, 0)
        ok = ok & (col <= row)
    return jnp.where(ok, s, -1e30)


def probs_of(q, key, i, rows, length, scale):
    parts = [masked_scores(q, key[j], i, j, rows, length, scale) for j in range(i + 1)]
    peak = parts[0].max(axis=1, keepdims=True)
    for s in parts[1:]:
        peak = jnp.maximum(peak, s.max(axis=1, keepdims=True))
    parts = [jnp.exp(s - peak) for s in parts]
    total = parts[0].sum(axis=1, keepdims=True)
    for e in parts[1:]:
        total = total + e.sum(axis=1, keepdims=True)
    inverse = 1.0 / total
    return [e * inverse for e in parts]


def turned(v, cosine, sine):
    return v * cosine + pltpu.roll(v, HEAD_DIM // 2, 1) * sine


def normed_turned(raw, factor, gain, cosine, sine):
    return turned(raw * factor * gain, cosine, sine).astype(BF)


def attend_kernel(inv, lens, q_ref, k_ref, v_ref, fac_ref, qg_ref, kg_ref, cos_ref, sin_ref, o_ref, key, *, first, blocks, rows, scale):
    length = lens[first + pl.program_id(0)]
    for i in range(blocks):
        at = inv[i]
        fac, cosine, sine = fac_ref[at], cos_ref[at], sin_ref[at]
        q = normed_turned(q_ref[at], fac[:, 0:1], qg_ref[...], cosine, sine)
        key[i] = normed_turned(k_ref[at], fac[:, 1:2], kg_ref[...], cosine, sine)
        probs = probs_of(q, key, i, rows, length, scale)
        out = jnp.zeros((rows, HEAD_DIM), F32)
        for j, p in enumerate(probs):
            out = out + dot(p.astype(BF), v_ref[inv[j]].astype(BF))
        o_ref[i] = out.astype(BF)


def attend_back_kernel(
    inv, lens, q_ref, k_ref, v_ref, fac_ref, qg_ref, kg_ref, cos_ref, sin_ref, do_ref,
    dq_ref, dk_ref, dv_ref, stat_ref, gain_ref, key, dk_acc, dv_acc, *, first, blocks, rows, scale
):
    length = lens[first + pl.program_id(0)]
    head = pl.program_id(1)
    dk_acc[...] = jnp.zeros_like(dk_acc)
    dv_acc[...] = jnp.zeros_like(dv_acc)

    @pl.when(head == 0)
    def _():
        stat_ref[...] = jnp.zeros_like(stat_ref)

    def unturn(at, grad, raw_ref, which, gain, out_ref):
        grad = turned(grad * scale, cos_ref[at], -sin_ref[at])
        out_ref[at] = grad
        weighted = grad * (raw_ref[at] * fac_ref[at][:, which : which + 1])
        stat_ref[at, :, which : which + 1] += jnp.sum(weighted * gain, axis=1, keepdims=True)
        return jnp.sum(weighted, axis=0, keepdims=True)

    qg, kg = qg_ref[...], kg_ref[...]
    dqg = jnp.zeros((1, HEAD_DIM), F32)
    dkg = jnp.zeros((1, HEAD_DIM), F32)
    for i in range(blocks):
        at = inv[i]
        fac, cosine, sine = fac_ref[at], cos_ref[at], sin_ref[at]
        q = normed_turned(q_ref[at], fac[:, 0:1], qg, cosine, sine)
        key[i] = normed_turned(k_ref[at], fac[:, 1:2], kg, cosine, sine)
        do = do_ref[i]
        probs = probs_of(q, key, i, rows, length, scale)
        dprobs = [dot(do, v_ref[inv[j]].astype(BF), NT) for j in range(i + 1)]
        delta = jnp.zeros((rows, 1), F32)
        for p, dp in zip(probs, dprobs):
            delta = delta + jnp.sum(p * dp, axis=1, keepdims=True)
        dq = jnp.zeros((rows, HEAD_DIM), F32)
        for j, (p, dp) in enumerate(zip(probs, dprobs)):
            ds = (p * (dp - delta)).astype(BF)
            dq = dq + dot(ds, key[j])
            dk_acc[j] += dot(ds, q, TN)
            dv_acc[j] += dot(p.astype(BF), do, TN)
        dqg = dqg + unturn(at, dq, q_ref, 0, qg, dq_ref)
    for j in range(blocks):
        at = inv[j]
        dkg = dkg + unturn(at, dk_acc[j], k_ref, 1, kg, dk_ref)
        dv_ref[at] = dv_acc[j].astype(BF)
    gain_ref[0:1, :] = dqg
    gain_ref[1:2, :] = dkg


def attention_call(lens, raw, factor, query_g, key_g, cosine, sine, first, seqs, inverse, grad=None):
    blocks, _, rows, width = raw.shape
    heads = width // (3 * HEAD_DIM)
    part = lambda k: pl.BlockSpec((blocks, None, rows, HEAD_DIM), lambda s, h, *_: (0, first + s, 0, k * heads + h))
    out = pl.BlockSpec((blocks, None, rows, HEAD_DIM), lambda s, h, *_: (0, s, 0, h))
    fac = pl.BlockSpec((blocks, None, rows, 2), lambda s, h, *_: (0, first + s, 0, 0))
    gain = pl.BlockSpec((1, HEAD_DIM), lambda s, h, *_: (0, h))
    turn = pl.BlockSpec((blocks, rows, HEAD_DIM), lambda s, h, *_: (0, 0, 0))
    ins = [raw, raw, raw, factor, query_g, key_g, cosine, sine]
    in_specs = [part(0), part(1), part(2), fac, gain, gain, turn, turn]
    one = (blocks, seqs, rows, width // 3)
    shape = jax.ShapeDtypeStruct
    scratch = [pltpu.VMEM((blocks, rows, HEAD_DIM), BF)]
    flops = 2 * 2 * (blocks * rows) ** 2 * seqs * width // 3 * 5 // 8
    if grad is None:
        kernel, outs, out_specs = attend_kernel, [shape(one, BF)], [out]
    else:
        ins, in_specs = ins + [grad], in_specs + [out]
        kernel = attend_back_kernel
        outs = [shape(one, F32), shape(one, F32), shape(one, BF)]
        outs += [shape((blocks, seqs, rows, 2), F32), shape((seqs, 2, width // 3), F32)]
        out_specs = [out] * 3 + [fac, pl.BlockSpec((None, 2, HEAD_DIM), lambda s, h, *_: (s, 0, h))]
        scratch += [pltpu.VMEM((blocks, rows, HEAD_DIM), F32)] * 2
        flops = flops * 5 // 2
    return pl.pallas_call(
        partial(kernel, first=first, blocks=blocks, rows=rows, scale=1.0 / math.sqrt(HEAD_DIM)),
        out_shape=outs,
        grid_spec=pltpu.PrefetchScalarGridSpec(
            num_scalar_prefetch=2, grid=(seqs, heads), in_specs=in_specs, out_specs=out_specs, scratch_shapes=scratch
        ),
        compiler_params=pltpu.CompilerParams(vmem_limit_bytes=VMEM_LIMIT),
        cost_estimate=pl.CostEstimate(
            flops=flops, bytes_accessed=raw.size * 6, transcendentals=(blocks * rows) ** 2 * seqs * heads * 5 // 8
        ),
    )(inverse, lens, *ins)


def pick_row(table, index):
    which = lax.broadcasted_iota(jnp.int32, table.shape, 0) == index
    return jnp.sum(jnp.where(which, table, 0.0), axis=0, keepdims=True)


def selection(rank_table, expert, cap):
    rank = pick_row(rank_table, expert)
    return lax.broadcasted_iota(jnp.int32, (cap, rank.shape[1]), 0).astype(F32) == rank


def dispatch(out, b, s, top, low, cap):
    half = top.shape[0]
    s = s.astype(F32).astype(BF)
    out[pl.ds(b * cap, cap), :] = (dot(s[:, :half], top[...]) + dot(s[:, half:], low[...])).astype(BF)


def experts_grad_kernel(base, *refs, cap, groups):
    pieces, wd, (og, dh) = refs[: 6 * groups], refs[6 * groups], refs[-2:]
    expert = base[1] + pl.program_id(0)
    for k in range(groups):

        @pl.when(pl.program_id(1) == k)
        def _():
            c00, c01, c10, c11, r0, r1 = pieces[6 * k : 6 * k + 6]
            for b, (r, top, low) in enumerate(((r0, c00, c01), (r1, c10, c11))):
                dispatch(og, b, selection(r[...], expert, cap), top, low, cap)

    ff = wd.shape[0]
    for at in range(0, ff, 512):
        cols = slice(at, min(at + 512, ff))
        dh[:, cols] = dot(og[...], wd[cols, :], NT)


def experts_in_kernel(base, *refs, cap, groups):
    pieces, (dhu, wg, wu) = refs[: 8 * groups], refs[8 * groups : 8 * groups + 3]
    buf, hg, dg, du, gg, weight, dots = refs[-7:]
    expert = base[1] + pl.program_id(0)
    for k in range(groups):

        @pl.when(pl.program_id(1) == k)
        def _():
            f00, f01, f10, f11, r0, r1, g0, g1 = pieces[8 * k : 8 * k + 8]
            for b, (r, g, top, low) in enumerate(((r0, g0, f00, f01), (r1, g1, f10, f11))):
                s = selection(r[...], expert, cap)
                dispatch(buf, b, s, top, low, cap)
                gate = pick_row(g[...], expert)
                weight[pl.ds(b * cap, cap), :] = jnp.sum(jnp.where(s, gate, 0.0), axis=1, keepdims=True)

    ff = wg.shape[1]
    total = None
    for at in range(0, ff, 512):
        cols = slice(at, min(at + 512, ff))
        x = buf[...]
        gate = dot(x, wg[:, cols])
        up = dot(x, wu[:, cols])
        dh = dhu[:, cols]
        w = weight[...]
        sg = 1.0 / (1.0 + jnp.exp(-gate))
        silu = gate * sg
        hidden = (silu * up).astype(BF).astype(F32)
        part = jnp.sum(hidden * dh, axis=1, keepdims=True)
        total = part if total is None else total + part
        dh = dh * w
        hg[:, cols] = (hidden * w).astype(BF)
        dg[:, cols] = (dh * up * (sg * (1.0 + gate * (1.0 - sg)))).astype(BF)
        du[:, cols] = (dh * silu).astype(BF)
    dots[...] = total
    for k in range(groups):

        @pl.when(pl.program_id(1) == k)
        def _():
            for b, r in enumerate(pieces[8 * k + 4 : 8 * k + 6]):
                s = selection(r[...], expert, cap)
                gg[b] = jnp.sum(jnp.where(s, dots[pl.ds(b * cap, cap), :], 0.0), axis=0, keepdims=True)


def experts_call(kernel, first, total, base, small, wide_ins, weights, wide_outs, gates, cap, local, before, flops):
    groups = len(small)
    width = weights[-1].shape[1] if gates else weights[-1].shape[2]
    ff = weights[-1].shape[2] if gates else weights[-1].shape[1]
    rows = 2 * cap
    tokens = small[0][0].shape[0] * 2
    small = [a for group in small for a in group]
    whole = lambda a: pl.BlockSpec(a.shape, lambda e, g, s: (0, 0), pipeline_mode=pl.Buffered(1))
    wide = pl.BlockSpec((None, rows, width), lambda e, g, s: (e, first + g, 0))
    thin = pl.BlockSpec((None, rows, ff), lambda e, g, s: (e, first + g, 0))
    heavy = pl.BlockSpec((None, *weights[-1].shape[1:]), lambda e, g, s: (s[0] + e, 0, 0))
    shape = jax.ShapeDtypeStruct
    outs = [shape((local, total * rows, width if w else ff), t) for w, t in wide_outs]
    out_specs = [wide if w else thin for w, _ in wide_outs]
    scratch = []
    if gates:
        outs.append(shape((local, groups, 2, 1, tokens), F32))
        out_specs.append(pl.BlockSpec((None, None, 2, 1, tokens), lambda e, g, s: (e, g, 0, 0, 0)))
        scratch = [pltpu.VMEM((rows, 1), F32)] * 2
    before = [] if before is None else before
    n = 1 + len(small) + len(wide_ins) + len(weights)
    return pl.pallas_call(
        partial(kernel, cap=cap, groups=groups),
        out_shape=outs,
        grid_spec=pltpu.PrefetchScalarGridSpec(
            num_scalar_prefetch=1,
            grid=(local, groups),
            in_specs=[whole(a) for a in small]
            + [thin] * len(wide_ins)
            + [heavy] * len(weights)
            + [pl.BlockSpec(memory_space=pl.ANY)] * len(before),
            out_specs=out_specs,
            scratch_shapes=scratch,
        ),
        input_output_aliases={n + i: i for i in range(len(before))},
        compiler_params=pltpu.CompilerParams(vmem_limit_bytes=VMEM_LIMIT),
        cost_estimate=pl.CostEstimate(
            flops=groups * flops,
            bytes_accessed=local * (len(weights) * width * ff * 2 + groups * rows * (2 * width + 10 * ff))
            + groups * 4 * tokens * width,
            transcendentals=groups * local * rows * ff if gates else 0,
        ),
    )(base, *small, *wide_ins, *weights, *before)


def experts_grad(first, total, base, small, wd, cap, local, before):
    flops = local * 2 * cap * wd.shape[2] * (2 * wd.shape[1] + 4 * small[0][0].shape[0])
    return experts_call(
        experts_grad_kernel, first, total, base, small, [], [wd], [(True, BF), (False, F32)],
        False, cap, local, before, flops,
    )


def experts_in(first, total, base, small, dhu, wg, wu, cap, local, before):
    flops = local * 2 * cap * wg.shape[1] * (4 * wg.shape[2] + 4 * small[0][0].shape[0])
    return experts_call(
        experts_in_kernel, first, total, base, small, [dhu], [wg, wu],
        [(True, BF), (False, BF), (False, BF), (False, BF)], True, cap, local, before, flops,
    )


def experts_out_kernel(base, *refs, cap, forward):
    if forward:
        hg, r0, r1, wd, t0, t1 = refs
        parts = [dot(hg[e], wd[e]).astype(BF) for e in range(hg.shape[0])]
    else:
        dg, du, r0, r1, wg, wu, t0, t1 = refs
        parts = [(dot(dg[e], wg[e], NT) + dot(du[e], wu[e], NT)).astype(BF) for e in range(dg.shape[0])]
    for b, (rank, final) in enumerate(((r0, t0), (r1, t1))):
        table = rank[...]
        total = None
        for e, part in enumerate(parts):
            which = lax.broadcasted_iota(jnp.int32, table.shape, 1) == base[1] + e
            column = jnp.sum(jnp.where(which, table, 0.0), axis=1, keepdims=True)
            slot = lax.broadcasted_iota(jnp.int32, (table.shape[0], cap), 1).astype(F32)
            pick = (slot == column).astype(F32).astype(BF)
            term = dot(pick, part[b * cap : (b + 1) * cap])
            total = term if total is None else total + term
        final[...] = total.astype(BF)


def experts_out(group, base, rows_in, ranks, weights, cap, local, forward):
    tokens = ranks[0].shape[0]
    width, ff = weights[0].shape[1:]
    if forward:
        ff, width = width, ff
    tile = 512
    rows = 2 * cap
    thin = pl.BlockSpec((local, rows, ff), lambda d, s: (0, group, 0))
    whole = pl.BlockSpec((tokens, EXPERTS), lambda d, s: (0, 0))
    final = pl.BlockSpec((tokens, tile), lambda d, s: (0, d))
    if forward:
        heavy = pl.BlockSpec((local, ff, tile), lambda d, s: (s[2], 0, d))
    else:
        heavy = pl.BlockSpec((local, tile, ff), lambda d, s: (s[2], d, 0))
    n = len(weights)
    return pl.pallas_call(
        partial(experts_out_kernel, cap=cap, forward=forward),
        out_shape=[jax.ShapeDtypeStruct((tokens, width), BF)] * 2,
        grid_spec=pltpu.PrefetchScalarGridSpec(
            num_scalar_prefetch=1,
            grid=(width // tile,),
            in_specs=[thin] * n + [whole] * 2 + [heavy] * n,
            out_specs=[final] * 2,
        ),
        compiler_params=pltpu.CompilerParams(vmem_limit_bytes=VMEM_LIMIT),
        cost_estimate=pl.CostEstimate(
            flops=local * rows * width * (2 * n * ff + 2 * tokens),
            bytes_accessed=local * n * (width * ff + rows * ff) * 2 + 4 * tokens * width,
            transcendentals=0,
        ),
    )(base, *rows_in, *ranks, *weights)


def shift(value, axis, by):
    n = lax.axis_size(axis)
    return lax.ppermute(value, axis, [(i, (i + by) % n) for i in range(n)])


def gather_small(value, axis):
    n, index, rows = lax.axis_size(axis), lax.axis_index(axis), value.shape[0]
    out = jnp.zeros((n * rows, *value.shape[1:]), value.dtype)
    for by in range(n):
        piece = shift(value, axis, by) if by else value
        out = lax.dynamic_update_slice_in_dim(out, piece, (index - by) % n * rows, 0)
    return out


def scatter_small(value, axis):
    n, index = lax.axis_size(axis), lax.axis_index(axis)
    value = value.reshape(n, -1, *value.shape[1:])
    part = lambda i: lax.dynamic_index_in_dim(value, i % n, 0, keepdims=False)
    total = part(index)
    for by in range(1, n):
        total = total + shift(part(index + by), axis, by)
    return total


def tie(*values):
    return lax.optimization_barrier(values)


def add_low(*terms):
    total = terms[0].astype(F32)
    for t in terms[1:]:
        total = total + t.astype(F32)
    return total.astype(BF)


def rms_parts(values):
    return values * lax.rsqrt(jnp.mean(values * values, axis=-1, keepdims=True) + EPS)


def local(
    nx,
    tokens,
    lengths,
    routes,
    w_query,
    w_key,
    w_value,
    w_out,
    w_router,
    attn_gain,
    query_gain,
    key_gain,
    ffn_gain,
    w_gate,
    w_up,
    w_down,
    cotangent,
):
    ALL, GROUP = ("r", "y", "x", "c"), ("x", "c")
    r, y, x, c = (lax.axis_index(a) for a in ALL)
    nr = lax.axis_size("r")
    me = 2 * x + c
    ng = 2 * nx
    seqs, span, width = tokens.shape
    token_count = seqs * span
    top_count = routes.shape[-1]
    cap = (token_count * top_count * 9 + 8 * EXPERTS - 1) // (8 * EXPERTS)
    cols = width // ng
    length = span * ng
    places = [(dx, dc) for dx in range(nx) for dc in range(2)]
    owner = jnp.stack([2 * ((x - dx) % nx) + (c - dc) % 2 for dx, dc in places]).astype(jnp.int32)
    inverse = jnp.stack(
        [2 * ((x - j // 2) % nx) + (c - j % 2) % 2 for j in range(ng)]
    ).astype(jnp.int32)

    w3 = jnp.stack([w_query, w_key, w_value], axis=1).reshape(-1, 3, ng, cols)
    w3 = w3.transpose(2, 0, 1, 3).reshape(ng, -1, 3 * cols)
    w3 = lax.all_to_all(w3, GROUP, split_axis=0, concat_axis=0, tiled=True)
    w3 = lax.all_gather(w3.reshape(-1, 3 * cols), ("r", "y"), axis=0, tiled=True)
    extras = jnp.concatenate(
        [w_router, attn_gain[:, None], query_gain[:, None], key_gain[:, None], ffn_gain[:, None]], axis=1
    )
    for axis in reversed(ALL):
        extras = gather_small(extras, axis)
    out_full = lax.all_gather(w_out, ALL, axis=0, tiled=True)
    router_full = extras[:, :EXPERTS]
    attn_g, query_g, key_g, ffn_g = (extras[:, EXPERTS + i].astype(F32) for i in range(4))
    query_g = lax.dynamic_slice(query_g, (me * cols,), (cols,))
    key_g = lax.dynamic_slice(key_g, (me * cols,), (cols,))

    choose = routes.reshape(token_count, top_count)
    chosen = jnp.sum(
        (choose[:, :, None] == jnp.arange(EXPERTS, dtype=jnp.int32)).astype(F32), axis=1
    )
    tri = (
        lax.broadcasted_iota(jnp.int32, (token_count, token_count), 0)
        > lax.broadcasted_iota(jnp.int32, (token_count, token_count), 1)
    ).astype(BF)
    rank = jnp.where(chosen > 0, dot(tri, chosen.astype(BF)), -1.0)

    def gather_group(value):
        pieces = []
        for dx in range(nx):
            far = shift(value, "x", dx) if dx else value
            pieces += [far, shift(far, "c", 1)]
        return pieces

    own_places = me * span + jnp.arange(span, dtype=jnp.int32)
    valid = (own_places[None, :] < lengths[:, None]).reshape(token_count)
    own_cot = jnp.where(valid[:, None], cotangent.reshape(token_count, width), jnp.zeros((), BF))
    own_tokens = tokens.astype(F32).reshape(token_count, width)

    all_tokens = jnp.stack(gather_group(tokens)).reshape(ng * token_count, width).astype(F32)
    h = token_count // 2
    cot_halves = [own_cot[:h], own_cot[h:]]
    near = [{dx: shift(v, "x", dx) if dx else v for dx in range(nx)} for v in cot_halves]
    normed_n = rms_parts(all_tokens)
    normed = (normed_n * attn_g).astype(BF)

    spots = [(dy, dx) for dy in range(2) for dx in range(nx)]

    def gather_pair(value):
        out = {(0, 0): value}
        for dx in range(1, nx):
            out[0, dx] = shift(value, "x", dx)
        for dx in range(nx):
            out[1, dx] = shift(out[0, dx], "y", 1)
        return {(dy, dx, dc): shift(v, "c", 1) if dc else v for (dy, dx), v in out.items() for dc in range(2)}

    def with_core(pieces):
        return pieces | {(dy, dx, 1): shift(v, "c", 1) for (dy, dx, _), v in pieces.items()}

    ranks_t = gather_pair(rank.T)
    ranks = {k: v.T for k, v in ranks_t.items()}
    w3, normed, ranks_t, near[0] = tie(w3, normed, ranks_t, near[0])

    local_experts = w_gate.shape[0]
    mine = local_experts // 2
    base = jnp.stack([y * mine, me * local_experts + y * mine, y]).astype(jnp.int32)
    both = lambda halves, dy, dx: [halves[h][dy, dx, dc] for dc in range(2) for h in range(2)]
    pair = lambda table, dy, dx: [table[dy, dx, dc] for dc in range(2)]

    close, far = spots[:nx], spots[nx:]

    def cot_call(chips, base, before):
        small = [[*both(cots, *k), *pair(ranks_t, *k)] for k in chips]
        return experts_grad(spots.index(chips[0]), len(spots), base, small, w_down, cap, mine, before)

    def in_call(chips, base, before):
        small = [[*both(feats, *k), *pair(ranks_t, *k), *pair(gates_t, *k)] for k in chips]
        return experts_in(spots.index(chips[0]), len(spots), base, small, dhu, w_gate, w_up, cap, mine, before)

    def sum_group(stats):
        stats = stats.reshape(2, ng, token_count)
        stats = jnp.concatenate([lax.dynamic_slice_in_dim(stats, inverse[j], 1, 1) for j in range(ng)], 1)
        stats = lax.psum(stats, GROUP)
        stats = jnp.concatenate([lax.dynamic_slice_in_dim(stats, owner[p], 1, 1) for p in range(ng)], 1)
        return stats.reshape(2, ng * token_count)

    starts = [n[0] for n in near]
    raw = dot(normed, w3)
    squares = jnp.stack(
        [jnp.sum(raw[:, i * cols : (i + 1) * cols] ** 2, -1) for i in range(2)]
    )
    across = [shift(v, "y", 1) for v in starts]
    squares, near[1] = tie(squares, near[1])
    squares = sum_group(squares)
    factor = lax.rsqrt(squares / width + EPS).T

    half = HEAD_DIM // 2
    frequencies = jnp.exp(jnp.arange(half, dtype=F32) * (-2.0 * math.log(10000.0) / HEAD_DIM))
    spot = owner[:, None] * span + jnp.arange(span, dtype=jnp.int32)[None, :]
    angles = spot.astype(F32)[:, :, None] * frequencies
    cosine, sine = jnp.cos(angles), jnp.sin(angles)
    cosine = jnp.concatenate([cosine, cosine], -1)
    sine = jnp.concatenate([-sine, sine], -1)
    attention = partial(
        attention_call,
        lengths,
        raw.reshape(ng, seqs, span, -1),
        factor.reshape(ng, seqs, span, 2),
        query_g[None],
        key_g[None],
        cosine,
        sine,
    )
    second, across[0] = tie(inverse, across[0])
    in_turn = [inverse, second]
    mixed = [attention(i, 1, inverse=in_turn[i])[0].reshape(ng, span, cols) for i in range(seqs)]
    mixed = [lax.all_to_all(a, GROUP, split_axis=0, concat_axis=0, tiled=True) for a in mixed]
    mixed[0], across[1] = tie(mixed[0], across[1])
    corner = [[shift(near[0][dx], "y", 1) for dx in range(1, nx)], [shift(across[1], "x", dx) for dx in range(1, nx)]]
    mixed[1], corner = tie(mixed[1], corner)
    cots = [{(0, dx, 0): v for dx, v in n.items()} for n in near]
    for i in range(2):
        cots[i][1, 0, 0] = across[i]
        for dx in range(1, nx):
            cots[i][1, dx, 0] = corner[i][dx - 1]
    cots = [with_core(p) for p in cots]
    cot_terms = cot_call(close, base, None)
    parts = []
    for i in range(seqs):
        a = mixed[i].transpose(1, 0, 2).reshape(span, width)
        u = tokens[i].astype(F32) + dot(a, out_full)
        q = lax.rsqrt(jnp.mean(u * u, axis=-1, keepdims=True) + EPS)
        f = (u * q * ffn_g).astype(BF)
        logits = dot(f, router_full)
        weights = jnp.exp(logits - jnp.max(logits, axis=-1, keepdims=True))
        parts.append((a, u, q, f, weights / jnp.sum(weights, axis=-1, keepdims=True)))
    attended, resid, ffn_scale, ffn_in, router = (jnp.concatenate(p, axis=0) for p in zip(*parts))
    ffn_n = resid * ffn_scale

    feats = [{(0, 0, 0): p[3]} for p in parts]
    for i in range(2):
        for dx in range(1, nx):
            feats[i][0, dx, 0] = shift(feats[i][0, 0, 0], "x", dx)
        feats[i][1, 0, 0] = shift(feats[i][0, 0, 0], "y", 1)
        if i == 0:
            row = [feats[0][k] for k in feats[0]]
            row, feats[1][0, 0, 0] = tie(row, feats[1][0, 0, 0])
            feats[0] = dict(zip(feats[0], row))
    base_at, feats[1][0, 0, 0] = tie(base, feats[1][0, 0, 0])
    cot_terms = cot_call(far, base_at, cot_terms)
    for dx in range(1, nx):
        feats[0][1, dx, 0] = shift(feats[0][0, dx, 0], "y", 1)
        feats[1][1, dx, 0] = shift(feats[1][1, 0, 0], "x", dx)
    gates_t = gather_pair(router.T)

    base_at, cot_terms = tie(base, cot_terms)
    og, dhu = cot_terms
    feats = [with_core(p) for p in feats]
    *before, gg = in_call(close, base_at, None)
    gate_terms = dict(zip(close, [gg[:, k] for k in range(nx)]))
    row = [[p[k] for k in p] for p in feats]
    base_at, row, before = tie(base_at, row, before)
    feats = [dict(zip(p, v)) for p, v in zip(feats, row)]
    *before, gg = in_call(far, base_at, before)
    gate_terms |= dict(zip(far, [gg[:, k] for k in range(nx)]))
    buf, hg, dg, du = before

    def weight_grad(left, right):
        return lax.dot_general(
            left, right, (((1,), (1,)), ((0,), (0,))), preferred_element_type=F32
        ).astype(BF)

    def finish_part(part):
        rows = part.shape[1] // 2
        keep = lax.dynamic_slice_in_dim(part, y * rows, rows, 1)
        give = shift(lax.dynamic_slice_in_dim(part, (1 - y) * rows, rows, 1), "y", 1)
        return keep, give

    def finish_grad(keep, give):
        first = jnp.where(y == 0, keep, give)
        second = jnp.where(y == 0, give, keep)
        return jnp.concatenate([first, second], axis=0).astype(F32)

    def over_r(value, dim):
        return lax.psum_scatter(value, "r", scatter_dimension=dim, tiled=True)

    first_full, at = tie(weight_grad(og, hg), base)
    scattered = [over_r(first_full, 1)]

    order = list(reversed(list(enumerate(spots))))
    both_ranks = lambda spot: [ranks[*spot, dc] for dc in range(2)]
    top = lambda v: v[:h]
    low = lambda v: v[h:]

    def core_sum(pair):
        return add_low(pair[0], shift(pair[1], "c", 1))

    def first_hops(acc):
        over_x = [shift(top(acc[1, dx]), "x", -dx) for dx in range(1, nx)]
        over_y = [shift(low(acc[1, dx]), "y", 1) for dx in range(1, nx)]
        return over_x, over_y

    def direct(acc):
        return [shift(top(acc[0, dx]), "x", -dx) for dx in range(1, nx)], shift(low(acc[1, 0]), "y", 1)

    def last_hops(acc, hops):
        far = shift(add_low(top(acc[1, 0]), *hops[0]), "y", 1)
        near = [shift(add_low(low(acc[0, dx]), hops[1][dx - 1]), "x", -dx) for dx in range(1, nx)]
        return far, near

    def arrived(acc, straight, last):
        total = lambda terms: sum(t.astype(F32) for t in terms)
        halves = total([top(acc[0, 0]), last[0], *straight[0]]), total([low(acc[0, 0]), straight[1], *last[1]])
        return jnp.concatenate(halves, axis=0)

    back = {}
    for i, (g, spot) in enumerate(order):
        if i >= 2:
            before_last = order[i - 2][1]
            at, back[before_last] = tie(at, back[before_last])
        terms = experts_out(g, at, [dg, du], both_ranks(spot), [w_gate, w_up], cap, mine, False)
        at, terms = tie(at, terms)
        back[spot] = core_sum(terms)
    dg, at = tie(dg, at)
    hops = first_hops(back)
    full = weight_grad(buf, dg)
    full, du, hops = tie(full, du, hops)
    straight = direct(back)
    at, straight = tie(base, straight)
    mix = {}

    def mix_group(i, at):
        g, spot = order[i]
        mix[spot] = experts_out(g, at, [hg], both_ranks(spot), [w_down], cap, mine, True)
        at, mix[spot] = tie(at, mix[spot])
        return at

    last = last_hops(back, hops)
    for i in range(len(order)):
        if i == 1:
            at, full, scattered[0] = tie(at, full, scattered[0])
            scattered.append(over_r(full, 1))
        if i == len(order) // 2:
            at, last = tie(at, last)
        at = mix_group(i, at)
    dffn = arrived(back, straight, last)

    def parts_y(part):
        return [lax.dynamic_index_in_dim(part, i, 1, keepdims=False) for i in (y, 1 - y)]

    def swap_y(part):
        keep, give = parts_y(part)
        return keep, shift(give, "y", 1)

    terms = jnp.stack([gate_terms[k] for k in spots])
    terms = terms.reshape(2, nx, mine, 2, token_count)
    pieces = []
    for k in range(2 * ng):
        ty, tx, tc = k // ng, (k % ng) // 2, k % 2
        piece = lax.dynamic_slice(
            terms, ((y - ty) % 2, (x - tx) % nx, 0, (c - tc) % 2, 0), (1, 1, mine, 1, token_count)
        )
        pieces.append(piece.reshape(mine, token_count))
    terms = lax.all_to_all(jnp.stack(pieces), ("y", "x", "c"), split_axis=0, concat_axis=0, tiled=True)
    drouter = terms.reshape(2, ng, mine, token_count).transpose(1, 0, 2, 3).reshape(EXPERTS, token_count).T

    dlogits = router * (drouter - jnp.sum(router * drouter, axis=-1, keepdims=True))
    highest = lax.Precision.HIGHEST
    grad_router = lax.dot_general(ffn_in.astype(F32), dlogits, (((0,), (0,)), ((), ())), precision=highest)
    dffn = dffn + lax.dot_general(
        dlogits, router_full.astype(F32), (((1,), (1,)), ((), ())), precision=highest
    )
    grad_ffn_g = jnp.sum(dffn * ffn_n, axis=0)
    gd = dffn * ffn_g
    dresid = own_cot.astype(F32) + ffn_scale * (gd - ffn_n * jnp.mean(gd * ffn_n, axis=-1, keepdims=True))

    dattn, mix = tie(dresid.astype(BF), mix)
    mix = {k: core_sum(v) for k, v in mix.items()}
    dattended = dot(dattn, out_full, NT).astype(BF)
    dattended = dattended.reshape(token_count, ng, cols).transpose(1, 0, 2).reshape(ng, seqs, span, cols)
    du, dattended = tie(du, dattended)
    dattended = lax.all_to_all(dattended, GROUP, split_axis=0, concat_axis=0, tiled=True)
    full = weight_grad(buf, du)
    grad_out = dot(attended, dattn, TN).astype(BF)
    wrows = w_out.shape[0]
    go = grad_out.reshape(nr * 2, nx, 2, wrows, width)
    keep = lax.dynamic_index_in_dim(go, c, 2, keepdims=False)
    give = lax.dynamic_index_in_dim(go, 1 - c, 2, keepdims=False)
    go = add_low(keep, shift(give, "c", 1))
    parted = [finish_part(scattered[0])]
    hops, straight = first_hops(mix), direct(mix)
    dattended, go, full, scattered[1] = tie(dattended, go, full, scattered[1])
    scattered.append(over_r(full, 1))
    dattended, hops, straight = tie(dattended, hops, straight)
    last = last_hops(mix, hops)
    dquery, dkey, dvalue, means, gain_grads = attention(0, seqs, inverse, dattended)

    go = add_low(
        *[
            shift(lax.dynamic_index_in_dim(go, (x + dx) % nx, 1, keepdims=False), "x", dx)
            if dx
            else lax.dynamic_index_in_dim(go, x, 1, keepdims=False)
            for dx in range(nx)
        ]
    )
    parted.append(finish_part(scattered[1]))
    dvalue, means, go, parted, last = tie(dvalue.reshape(-1, cols), means, go, parted, last)
    output = (resid + arrived(mix, straight, last)).astype(BF).reshape(seqs, span, width)
    g_value, means = tie(dot(normed, dvalue, TN).astype(BF), means)
    thirds = [swap_y(g_value.reshape(nr, 2, -1, cols))]
    means = sum_group(means.reshape(-1, 2).T).T / width
    gain_grads = gain_grads.sum(axis=0)
    grad_query_g, grad_key_g = gain_grads[0], gain_grads[1]

    def raw_grad(grad, i, gain):
        n = raw[:, i * cols : (i + 1) * cols] * factor[:, i : i + 1]
        return (factor[:, i : i + 1] * (grad.reshape(-1, cols) * gain - n * means[:, i : i + 1])).astype(BF)

    draws = [raw_grad(dquery, 0, query_g), raw_grad(dkey, 1, key_g), dvalue]
    g_pair = dot(normed, jnp.concatenate(draws[:2], axis=1), TN).astype(BF)
    keep, give = parts_y(g_pair.reshape(nr, 2, -1, 2 * cols))
    keep, give, thirds[0], draws = tie(keep, give, thirds[0], draws)
    thirds.append((keep, shift(give, "y", 1)))
    draw = jnp.concatenate(draws, axis=1)
    dnormed = dot(draw, w3, NT)
    grad_attn_g = jnp.sum(dnormed * normed_n, axis=0)
    g_value, scattered[2] = tie(add_low(*thirds[0]), scattered[2])
    g_value = over_r(g_value, 0)
    spread = lambda v: lax.dynamic_update_slice(jnp.zeros((width,), F32), v, (me * cols,))
    sums = jnp.concatenate(
        [
            grad_router,
            grad_attn_g[:, None],
            spread(grad_query_g)[:, None],
            spread(grad_key_g)[:, None],
            grad_ffn_g[:, None],
        ],
        axis=1,
    )
    sums = scatter_small(sums, "r")
    dnormed, thirds[1], go, sums, g_value = tie(dnormed.astype(BF), thirds[1], go, sums, g_value)
    go = add_low(*swap_y(go.reshape(nr, 2, wrows, width)))
    thirds[1] = add_low(*thirds[1])
    sums = scatter_small(sums, "y")
    dnormed = dnormed.reshape(nx, 2, token_count, width)
    dnormed = [add_low(dnormed[dx, 0], shift(dnormed[dx, 1], "c", 1)) for dx in range(nx)]
    dnormed = sum(
        (shift(dnormed[dx], "x", -dx) if dx else dnormed[0]).astype(F32) for dx in range(nx)
    )
    own_scale = lax.rsqrt(jnp.mean(own_tokens * own_tokens, axis=-1, keepdims=True) + EPS)
    own_n = own_tokens * own_scale
    gd = dnormed * attn_g
    grad_input = dresid + own_scale * (gd - own_n * jnp.mean(gd * own_n, axis=-1, keepdims=True))
    grad_input = grad_input.reshape(seqs, span, width)

    g_pair, go, scattered[2], sums = tie(over_r(thirds[1], 0), go, scattered[2], sums)
    go = over_r(go, 0)
    for axis in ("x", "c"):
        sums = scatter_small(sums, axis)
    parted.append(finish_part(scattered[2]))
    g_pair = g_pair.reshape(ng, wrows, 2, cols)
    g_value = g_value.reshape(ng, wrows, 1, cols)
    go = go.reshape(wrows, width).astype(F32)
    g3 = jnp.concatenate([g_pair, g_value], axis=2).transpose(2, 0, 1, 3)
    g3 = lax.all_to_all(g3, GROUP, split_axis=1, concat_axis=1, tiled=True)
    g3 = g3.transpose(0, 2, 1, 3).reshape(3, wrows, width).astype(F32)
    grad_down, grad_gate, grad_up = (finish_grad(*p) for p in parted)
    grad_down = grad_down.transpose(0, 2, 1)

    return (
        output,
        grad_input,
        g3[0],
        g3[1],
        g3[2],
        go,
        sums[:, :EXPERTS],
        sums[:, EXPERTS],
        sums[:, EXPERTS + 1],
        sums[:, EXPERTS + 2],
        sums[:, EXPERTS + 3],
        grad_gate,
        grad_up,
        grad_down,
    )


def solution(mesh):
    ndp, nex = mesh.shape["dp"], mesh.shape["expert"]
    nx = nex // 2
    fine = Mesh(mesh.devices.reshape(ndp // 2, 2, nx, 2), ("r", "y", "x", "c"))
    dp, ex = ("r", "y"), ("x", "c")
    both = dp + ex
    placed = (
        P(dp, ex, None),
        P(dp),
        P(dp, ex, None, None),
        P(both, None),
        P(both, None),
        P(both, None),
        P(both, None),
        P(both, None),
        P(both),
        P(both),
        P(both),
        P(both),
        P(ex, None, None),
        P(ex, None, None),
        P(ex, None, None),
        P(dp, ex, None),
    )
    return jax.shard_map(
        partial(local, nx),
        mesh=fine,
        in_specs=placed,
        out_specs=(
            P(dp, ex, None),
            P(dp, ex, None),
            P(both, None),
            P(both, None),
            P(both, None),
            P(both, None),
            P(both, None),
            P(both),
            P(both),
            P(both),
            P(both),
            P(ex, dp, None),
            P(ex, dp, None),
            P(ex, None, dp),
        ),
        check_vma=False,
    )
```
